32 devices in a mesh: clip: 8 (over z, y), frame: 4 (over x, core).
Axes of the slice: x: 2, y: 2, z: 4, core: 2. Of those that a mesh axis runs over, the one named last changes fastest.
Arguments:
- frames: bfloat16 [256, 16, 1152], P('clip', 'frame'), may hold values from -6 to 6
- conv_weight: bfloat16 [3, 1152, 1152], replicated, may hold values from -0.109375 to 0.109375
- captions: bfloat16 [256, 1152], P(('clip', 'frame')), may hold values from -6 to 6
- positive: int32 [256], P('clip'), may hold values from 0 to 255, as said below
Outputs:
- loss: float32 [], replicated
- grad_weight: float32 [3, 1152, 1152], P(None, 'clip', 'frame')
- grad_captions: float32 [256, 1152], P(('clip', 'frame'))
The draws below stay inside these ranges and needn't reach their ends.
Inputs may be any that keep to these rules, and one draw needn't show every extreme that they name: Each caption id is the positive of exactly one clip.
All inputs are finite; a program needn't handle non-finite values.
Results may differ from the reference program's by a relative error of at most 0.0028.
The reference program's roundings to bfloat16 on the way (of `u_low`, `v_low`, `coef` and `dconv`) count: a program that leaves them out, or rounds other values in their place, can miss the bound.
Values may be sent and summed in bfloat16 or wider, within the bound.
A program may use at most 128 MiB of HBM per device.

```python
import math
import jax
import jax.numpy as jnp
from jax import lax

D = 1152
FRAMES = 16
CLIPS = 256
CAPTIONS = 256


def pairing_order(key):
    return jax.random.permutation(jax.random.fold_in(key, 21), CLIPS).astype(jnp.int32)


def caption_base(key, topic_share, common_share):
    order = jax.random.permutation(jax.random.fold_in(key, 11), CAPTIONS).astype(jnp.int32)
    groups = order // 16
    topics = jax.random.normal(jax.random.fold_in(key, 12), (CAPTIONS // 16 + 1, D), jnp.float32)
    noise = jax.random.normal(jax.random.fold_in(key, 13), (CAPTIONS, D), jnp.float32)
    common = jax.random.normal(jax.random.fold_in(key, 14), (1, D), jnp.float32)
    rest = 1.0 - topic_share - common_share
    return math.sqrt(common_share) * common + math.sqrt(topic_share) * topics[groups] + math.sqrt(rest) * noise


def draw_positive(key, part):
    return pairing_order(key)


def draw_captions(key, part):
    topic_share, common_share = (0.7, 0.04)
    base = caption_base(key, topic_share, common_share)
    own = jax.random.fold_in(key, 7)
    scales = jnp.exp(jax.random.uniform(own, (CAPTIONS, 1), jnp.float32, -0.7, 0.7))
    return jnp.clip(base * scales, -6.0, 6.0).astype(jnp.bfloat16)


def draw_frames(key, part):
    topic_share, common_share = (0.7, 0.04)
    base = caption_base(key, topic_share, common_share)
    paired = base[pairing_order(key)]
    own = jax.random.fold_in(key, 3)
    noise = jax.random.normal(own, (CLIPS, FRAMES, D), jnp.float32)
    mixed = 0.8 * paired[:, None, :] + 0.6 * noise
    return jnp.clip(mixed, -6.0, 6.0).astype(jnp.bfloat16)


def centred(key, extent, deviation, bound, held_as=jnp.bfloat16):
    return jnp.clip(deviation * jax.random.normal(key, extent, jnp.float32), -bound, bound).astype(held_as)


def setup_inputs(seed: int = 0) -> dict:
    key_of = jax.random.split(jax.random.key(seed), 5)
    return {
        "frames": draw_frames(jax.random.fold_in(key_of[4], 71), 0),
        "conv_weight": centred(key_of[1], (3, D, D), (3 * D) ** -0.5, 0.109375),
        "captions": draw_captions(jax.random.fold_in(key_of[4], 71), 0),
        "positive": draw_positive(jax.random.fold_in(key_of[4], 71), 0),
    }


def reference(frames, conv_weight, captions, positive):
    clips, nframes, width = frames.shape
    padded = jnp.pad(frames, ((0, 0), (1, 1), (0, 0)))
    shifted = [padded[:, k:k + nframes].reshape(clips * nframes, width) for k in range(3)]
    conv = jnp.dot(shifted[0], conv_weight[0], preferred_element_type=jnp.float32)
    conv = conv + jnp.dot(shifted[1], conv_weight[1], preferred_element_type=jnp.float32)
    conv = conv + jnp.dot(shifted[2], conv_weight[2], preferred_element_type=jnp.float32)
    hidden = frames.reshape(clips * nframes, width).astype(jnp.float32) + jax.nn.gelu(conv)
    pooled = lax.optimization_barrier(jnp.mean(hidden.reshape(clips, nframes, width), axis=1))
    pnorm = jnp.sqrt(lax.optimization_barrier(jnp.sum(pooled * pooled, axis=1, keepdims=True)) + 1e-06)
    unit = pooled / pnorm
    u_low = unit.astype(jnp.bfloat16)
    capf = captions.astype(jnp.float32)
    cnorm = jnp.sqrt(lax.optimization_barrier(jnp.sum(capf * capf, axis=1, keepdims=True)) + 1e-06)
    vunit = capf / cnorm
    v_low = vunit.astype(jnp.bfloat16)
    logits = 10.0 * jnp.dot(u_low, v_low.T, preferred_element_type=jnp.float32) - 10.0
    ids = jnp.arange(captions.shape[0], dtype=jnp.int32)
    match = (positive[:, None] == ids[None, :]).astype(jnp.float32)
    sign = 2.0 * match - 1.0
    loss = jnp.sum(jax.nn.softplus(-sign * logits)) / clips
    coef = (10.0 * (jax.nn.sigmoid(logits) - match)).astype(jnp.bfloat16)
    du = jnp.dot(coef, v_low, preferred_element_type=jnp.float32)
    dv = jnp.dot(coef.T, u_low, preferred_element_type=jnp.float32)
    grad_captions = (dv - vunit * lax.optimization_barrier(jnp.sum(vunit * dv, axis=1, keepdims=True))) / cnorm
    dpooled = (du - unit * lax.optimization_barrier(jnp.sum(unit * du, axis=1, keepdims=True))) / pnorm
    dhidden = jnp.broadcast_to((dpooled / nframes)[:, None, :], (clips, nframes, width)).reshape(clips * nframes, width)
    _, pull = jax.vjp(jax.nn.gelu, conv)
    dconv = pull(dhidden)[0].astype(jnp.bfloat16)
    grads = [lax.dot_general(shifted[k], dconv, (((0,), (0,)), ((), ())), preferred_element_type=jnp.float32) for k in range(3)]
    return (loss, jnp.stack(grads), grad_captions)
```

```python
import functools
import math

import jax
import jax.numpy as jnp
from jax import lax
from jax.experimental import pallas as pl
from jax.experimental.pallas import tpu as pltpu
from jax.sharding import PartitionSpec as P

FRAMES = 16


def with_halo(block, sides, width):
    for axis, dim in sides:
        count = lax.axis_size(axis)
        forward = [(i, i + 1) for i in range(count - 1)]
        backward = [(target, source) for source, target in forward]
        low = lax.ppermute(
            lax.slice_in_dim(block, block.shape[dim] - width, None, axis=dim), axis, forward
        )
        high = lax.ppermute(lax.slice_in_dim(block, 0, width, axis=dim), axis, backward)
        block = jnp.concatenate([low, block, high], axis=dim)
    return block


def plain(frames, conv_weight, captions, positive):
    clip_dev, fr_dev, width = frames.shape
    rows = clip_dev * fr_dev
    padded = with_halo(frames, (("frame", 1),), 1)
    shifted = [padded[:, k : k + fr_dev].reshape(rows, width) for k in range(3)]
    conv = jnp.dot(shifted[0], conv_weight[0], preferred_element_type=jnp.float32)
    conv = conv + jnp.dot(shifted[1], conv_weight[1], preferred_element_type=jnp.float32)
    conv = conv + jnp.dot(shifted[2], conv_weight[2], preferred_element_type=jnp.float32)
    hidden = frames.reshape(rows, width).astype(jnp.float32) + jax.nn.gelu(conv)
    partial_pool = jnp.sum(hidden.reshape(clip_dev, fr_dev, width), axis=1)
    pooled = lax.psum(partial_pool, "frame") / FRAMES
    pnorm = jnp.sqrt(jnp.sum(pooled * pooled, axis=1, keepdims=True) + 1e-06)
    unit = pooled / pnorm
    u_low = unit.astype(jnp.bfloat16)
    capf = captions.astype(jnp.float32)
    cnorm = jnp.sqrt(jnp.sum(capf * capf, axis=1, keepdims=True) + 1e-06)
    vunit = capf / cnorm
    v_low = vunit.astype(jnp.bfloat16)
    cap_dev = captions.shape[0]
    frame_pos = lax.axis_index("frame")
    piece = lax.all_gather(v_low, "clip", axis=0, tiled=True)
    count = piece.shape[0]
    place = jnp.arange(count, dtype=jnp.int32)
    ids = place // cap_dev * clip_dev + frame_pos * cap_dev + place % cap_dev
    logits = (
        10.0
        * lax.dot_general(
            u_low, piece, (((1,), (1,)), ((), ())), preferred_element_type=jnp.float32
        )
        - 10.0
    )
    match = (positive[:, None] == ids[None, :]).astype(jnp.float32)
    sign = 2.0 * match - 1.0
    total = jnp.sum(jax.nn.softplus(-sign * logits))
    coef = (10.0 * (jax.nn.sigmoid(logits) - match)).astype(jnp.bfloat16)
    du_acc = jnp.dot(coef, piece, preferred_element_type=jnp.float32)
    dv_piece = lax.dot_general(
        coef, u_low, (((0,), (0,)), ((), ())), preferred_element_type=jnp.float32
    )
    total, du_part, dv_all = (total, du_acc, dv_piece)
    dv_mine = lax.psum_scatter(dv_all, "clip", scatter_dimension=0, tiled=True)
    grad_captions = (dv_mine - vunit * jnp.sum(vunit * dv_mine, axis=1, keepdims=True)) / cnorm
    loss = lax.psum(total, ("clip", "frame")) / (clip_dev * lax.axis_size("clip"))
    du_full = lax.psum(du_part, "frame")
    dpooled = (du_full - unit * jnp.sum(unit * du_full, axis=1, keepdims=True)) / pnorm
    dhidden = jnp.broadcast_to((dpooled / FRAMES)[:, None, :], (clip_dev, fr_dev, width)).reshape(
        rows, width
    )
    _, pull = jax.vjp(jax.nn.gelu, conv)
    dconv = pull(dhidden)[0].astype(jnp.bfloat16).reshape(clip_dev, fr_dev, width)
    dconv_cols = lax.all_to_all(dconv, "frame", split_axis=2, concat_axis=1, tiled=True)
    block = fr_dev + 2
    col_width = dconv_cols.shape[2]
    every_block = lax.all_gather(padded, "frame", axis=1, tiled=True)
    groups = every_block.shape[1] // block
    blocks = every_block.reshape(clip_dev, groups, block, width)
    grads = dconv_cols.reshape(clip_dev, groups, fr_dev, col_width)
    parts = [
        jnp.einsum(
            "cgtd,cgte->de", blocks[:, :, k : k + fr_dev], grads, preferred_element_type=jnp.float32
        )
        for k in range(3)
    ]
    terms = jnp.stack(parts)
    grad_weight = lax.psum_scatter(terms, "clip", scatter_dimension=1, tiled=True)
    return (loss, grad_weight, grad_captions)


MESH = pl.DeviceIdType.MESH


def remote(src, dst, send_sem, recv_sem, device):
    return pltpu.make_async_remote_copy(
        src_ref=src,
        dst_ref=dst,
        send_sem=send_sem,
        recv_sem=recv_sem,
        device_id=device,
        device_id_type=MESH,
    )


def nt_dot(a, b):
    return lax.dot_general(a, b, (((1,), (1,)), ((), ())), preferred_element_type=jnp.float32)


def ring_to_clip(r, count):
    high = r // (count // 2)
    return 2 * r + high * (2 * count - 1 - 4 * r)


def fused_kernel(
    C,
    F,
    frames_ref,
    w_hbm,
    cap_ref,
    pos_ref,
    loss_ref,
    gw_ref,
    gc_ref,
    w_ref,
    x_rows,
    xt,
    xu,
    x3,
    v32,
    vb,
    u32,
    ub,
    slope,
    dt,
    dbuf,
    acc,
    w_sem,
    fr_send,
    fr_recv,
    v1_send,
    v1_recv,
    v2_send,
    v2_recv,
    x1_send,
    x1_recv,
    x2_send,
    x2_recv,
    u1_send,
    u1_recv,
    u2_send,
    u2_recv,
    da_send,
    da_recv,
    ring_send,
    ring_recv,
):
    D = cap_ref.shape[1]
    NB = cap_ref.shape[0]
    T = FRAMES
    ROWS = T * NB
    part = ROWS // F
    RC = D // C
    CC = D // F
    c = lax.axis_index("clip")
    f = lax.axis_index("frame")
    half = C // 2
    z = c // 2
    pos = z + (c - 2 * z) * (C - 1 - 2 * z)
    right = ring_to_clip(lax.rem(pos + 1, C), C)
    left = ring_to_clip(lax.rem(pos + C - 1, C), C)

    w_copies = [pltpu.make_async_copy(w_hbm.at[k], w_ref.at[k], w_sem.at[k]) for k in range(3)]
    for copy in w_copies:
        copy.start()

    def cpeer(d):
        return lax.rem(c + d, C)

    def fpeer(d):
        return lax.rem(f + d, F)

    barrier = pltpu.get_barrier_semaphore()
    for d in range(1, C):
        pl.semaphore_signal(barrier, inc=1, device_id=(cpeer(d), f), device_id_type=MESH)
    for d in range(1, F):
        pl.semaphore_signal(barrier, inc=1, device_id=(c, fpeer(d)), device_id_type=MESH)
    pl.semaphore_wait(barrier, C + F - 2)

    sends = []

    def go(copy):
        copy.start()
        sends.append(copy)

    for d in range(1, F):
        go(
            remote(
                frames_ref.at[fpeer(d)],
                x_rows.at[f],
                fr_send.at[d],
                fr_recv.at[d],
                (c, fpeer(d)),
            )
        )
    x_rows[f] = frames_ref[f]

    capf = cap_ref[...].astype(jnp.float32)
    cnorm = jnp.sqrt(jnp.sum(capf * capf, axis=1, keepdims=True) + 1e-06)
    vunit = capf / cnorm
    v_own = vunit.astype(jnp.bfloat16)
    v32[c, f] = v_own.astype(jnp.float32)
    for d in range(1, C):
        go(remote(v32.at[c, f], v32.at[c, f], v1_send.at[d], v1_recv.at[d], (cpeer(d), f)))

    for d in range(1, F):
        source = fpeer(F - d)
        remote(
            x_rows.at[source], x_rows.at[source], fr_send.at[d], fr_recv.at[d], (c, source)
        ).wait_recv()
    xf = x_rows[...].reshape(ROWS, D).astype(jnp.float32)
    xt[...] = xf.T.astype(jnp.bfloat16).reshape(C, RC, ROWS)
    for d in range(1, C):
        to = cpeer(d)
        go(remote(xt.at[to], xu.at[c, f], x1_send.at[d], x1_recv.at[d], (to, f)))
    xu[c, f] = xt[c]

    edge = jnp.zeros((NB, D), jnp.float32)
    before = jnp.concatenate([edge, xf[: ROWS - NB]], axis=0).astype(jnp.bfloat16)
    after = jnp.concatenate([xf[NB:], edge], axis=0).astype(jnp.bfloat16)
    w_copies[0].wait()
    conv = jnp.dot(before, w_ref[0], preferred_element_type=jnp.float32)

    for d in range(1, C):
        source = cpeer(C - d)
        slot = v32.at[source, f]
        remote(slot, slot, v1_send.at[d], v1_recv.at[d], (source, f)).wait_recv()
    for d in range(1, F):
        slab = v32.at[:, f]
        go(remote(slab, slab, v2_send.at[d], v2_recv.at[d], (c, fpeer(d))))

    w_copies[1].wait()
    conv = conv + jnp.dot(
        x_rows[...].reshape(ROWS, D), w_ref[1], preferred_element_type=jnp.float32
    )
    w_copies[2].wait()
    conv = conv + jnp.dot(after, w_ref[2], preferred_element_type=jnp.float32)

    scale = math.sqrt(2.0 / math.pi)
    square = conv * conv
    tanh = jnp.tanh(scale * conv * (1.0 + 0.044715 * square))
    cdf = 0.5 * (1.0 + tanh)
    slope[...] = cdf + (0.5 * scale) * conv * (1.0 - tanh * tanh) * (1.0 + 0.134145 * square)
    hidden = xf + conv * cdf
    pooled = jnp.sum(hidden.reshape(T, NB, D), axis=0) * (1.0 / T)
    pnorm = jnp.sqrt(jnp.sum(pooled * pooled, axis=1, keepdims=True) + 1e-06)
    unit = pooled / pnorm
    u_low = unit.astype(jnp.bfloat16)
    pos_own = pos_ref[f]
    u32[c, f, :, :D] = u_low.astype(jnp.float32)
    u32[c, f, :, D:] = pos_own
    for d in range(1, C):
        go(remote(u32.at[c, f], u32.at[c, f], u1_send.at[d], u1_recv.at[d], (cpeer(d), f)))

    for d in range(1, F):
        slab = v32.at[:, fpeer(F - d)]
        remote(slab, slab, v2_send.at[d], v2_recv.at[d], (c, fpeer(F - d))).wait_recv()
    caps = C * F * NB
    vb[...] = v32[...].reshape(caps, D).astype(jnp.bfloat16)
    logits = 10.0 * nt_dot(u_low, vb[...]) - 10.0
    ids = lax.broadcasted_iota(jnp.int32, (NB, caps), 1).astype(jnp.float32)
    match = jnp.where(pos_own[:, :1] == ids, 1.0, 0.0)
    coef = (10.0 * (1.0 / (1.0 + jnp.exp(-logits)) - match)).astype(jnp.bfloat16)
    du = jnp.dot(coef, vb[...], preferred_element_type=jnp.float32)
    dpooled = (du - unit * jnp.sum(unit * du, axis=1, keepdims=True)) / pnorm
    step = dpooled * (1.0 / T)
    dconv = (slope[...].reshape(T, NB, D) * step[None]).reshape(ROWS, D)
    dt[...] = dconv.T.astype(jnp.bfloat16).reshape(F, CC, ROWS)
    for d in range(1, F):
        to = fpeer(d)
        go(remote(dt.at[to], dbuf.at[c, f], da_send.at[d], da_recv.at[d], (c, to)))
    dbuf[c, f] = dt[f]

    ways = (right, left)

    def block_at(way, hop):
        return ring_to_clip(lax.rem(pos + (C - hop if way == 0 else hop), C), C)

    def units_at(way, hop):
        if hop < half:
            return range(F)
        return range(F // 2) if way == 0 else range(F // 2, F)

    def forward(way, hop, q):
        slot = dbuf.at[block_at(way, hop), fpeer(F - q)]
        go(
            remote(
                slot,
                slot,
                ring_send.at[way, hop, q],
                ring_recv.at[way, hop, q],
                (ways[way], f),
            )
        )

    def arrive(way, hop, q):
        slot = dbuf.at[block_at(way, hop), fpeer(F - q)]
        remote(
            slot,
            slot,
            ring_send.at[way, hop - 1, q],
            ring_recv.at[way, hop - 1, q],
            (ways[way], f),
        ).wait_recv()

    def relay(hop):
        for q in range(F):
            for way in range(2):
                if q in units_at(way, hop):
                    arrive(way, hop, q)
                    if hop < half and q in units_at(way, hop + 1):
                        forward(way, hop, q)

    def add_block(block, first=False):
        rhs = jnp.concatenate([dbuf[block, i] for i in range(F)], axis=1)
        term = nt_dot(x3[block], rhs)
        if first:
            acc[...] = term
        else:
            acc[...] += term

    for q in range(F):
        if q:
            source = fpeer(F - q)
            slot = dbuf.at[c, source]
            remote(slot, slot, da_send.at[q], da_recv.at[q], (c, source)).wait_recv()
        for way in range(2):
            if q in units_at(way, 1):
                forward(way, 0, q)

    for d in range(1, C):
        source = cpeer(C - d)
        slot = xu.at[source, f]
        remote(slot, slot, x1_send.at[d], x1_recv.at[d], (source, f)).wait_recv()
    for d in range(1, F):
        slab = xu.at[:, f]
        go(remote(slab, slab, x2_send.at[d], x2_recv.at[d], (c, fpeer(d))))
    for d in range(1, C):
        source = cpeer(C - d)
        slot = u32.at[source, f]
        remote(slot, slot, u1_send.at[d], u1_recv.at[d], (source, f)).wait_recv()
    for d in range(1, F):
        slab = u32.at[:, f]
        go(remote(slab, slab, u2_send.at[d], u2_recv.at[d], (c, fpeer(d))))

    relay(1)
    for d in range(1, F):
        slab = xu.at[:, fpeer(F - d)]
        remote(slab, slab, x2_send.at[d], x2_recv.at[d], (c, fpeer(F - d))).wait_recv()
    row = lax.broadcasted_iota(jnp.int32, (ROWS, ROWS), 0)
    col = lax.broadcasted_iota(jnp.int32, (ROWS, ROWS), 1)
    later = jnp.where(row == col - NB, 1.0, 0.0)
    earlier = jnp.where(row == col + NB, 1.0, 0.0)
    moves = jnp.concatenate([later, earlier], axis=1).astype(jnp.bfloat16)

    def shift(block, carry):
        units = xu[block]
        moved = jnp.dot(
            units.reshape(F * RC, ROWS), moves, preferred_element_type=jnp.float32
        ).astype(jnp.bfloat16)
        for i in range(F):
            lanes = slice(i * ROWS, (i + 1) * ROWS)
            rows = slice(i * RC, (i + 1) * RC)
            x3[block, 0:RC, lanes] = moved[rows, :ROWS]
            x3[block, RC : 2 * RC, lanes] = units[i]
            x3[block, 2 * RC :, lanes] = moved[rows, ROWS:]
        return carry

    lax.fori_loop(0, C, shift, 0)
    add_block(c, first=True)

    relay(2)
    add_block(block_at(0, 1))
    add_block(block_at(1, 1))

    for d in range(1, F):
        slab = u32.at[:, fpeer(F - d)]
        remote(slab, slab, u2_send.at[d], u2_recv.at[d], (c, fpeer(F - d))).wait_recv()
    ub[...] = u32[:, :, :, :D].reshape(caps, D).astype(jnp.bfloat16)
    pos_all = u32[:, :, :, D:].reshape(caps, u32.shape[3] - D)
    pos_row = pos_all.T[:1]
    first_id = (c * F + f) * NB
    own_ids = (first_id + lax.broadcasted_iota(jnp.int32, (NB, caps), 0)).astype(jnp.float32)
    match_own = jnp.where(pos_row == own_ids, 1.0, 0.0)
    logits_own = 10.0 * nt_dot(v_own, ub[...]) - 10.0
    coef_own = (10.0 * (1.0 / (1.0 + jnp.exp(-logits_own)) - match_own)).astype(jnp.bfloat16)
    dv = jnp.dot(coef_own, ub[...], preferred_element_type=jnp.float32)
    gc_ref[...] = (dv - vunit * jnp.sum(vunit * dv, axis=1, keepdims=True)) / cnorm

    relay(3)
    add_block(block_at(0, 2))
    add_block(block_at(1, 2))

    every = 10.0 * nt_dot(ub[...], vb[...]) - 10.0
    all_ids = lax.broadcasted_iota(jnp.int32, (caps, caps), 1).astype(jnp.float32)
    signed = jnp.where(pos_all[:, :1] == all_ids, -every, every)
    soft = jnp.maximum(signed, 0.0) + jnp.log1p(jnp.exp(-jnp.abs(signed)))
    total = jnp.sum(jnp.sum(soft, axis=0, keepdims=True), axis=1, keepdims=True)
    loss_ref[...] = jnp.broadcast_to(total * (1.0 / caps), loss_ref.shape)

    add_block(block_at(0, 3))
    add_block(block_at(1, 3))
    relay(4)
    add_block(block_at(0, 4))
    gw_ref[...] = acc[...].reshape(3, RC, CC)
    for copy in sends:
        copy.wait_send()


def fused(C, F, frames, conv_weight, captions, positive):
    clip_dev, fr_dev, D = frames.shape
    NB = clip_dev // F
    ROWS = FRAMES * NB
    RC, CC = D // C, D // F
    half = C // 2
    blocks = frames.reshape(F, NB, fr_dev, D).transpose(0, 2, 1, 3).reshape(F, fr_dev * NB, D)
    ids = jnp.broadcast_to(positive.astype(jnp.float32).reshape(F, NB, 1), (F, NB, 128))
    vmem = pl.BlockSpec(memory_space=pltpu.VMEM)
    dma = pltpu.SemaphoreType.DMA
    bf16, f32 = jnp.bfloat16, jnp.float32
    caps = C * F * NB
    loss, grad_weight, grad_captions = pl.pallas_call(
        functools.partial(fused_kernel, C, F),
        out_shape=(
            jax.ShapeDtypeStruct((8, 128), f32),
            jax.ShapeDtypeStruct((3, RC, CC), f32),
            jax.ShapeDtypeStruct((NB, D), f32),
        ),
        in_specs=[vmem, pl.BlockSpec(memory_space=pl.ANY), vmem, vmem],
        out_specs=(vmem, vmem, vmem),
        scratch_shapes=[
            pltpu.VMEM((3, D, D), bf16),
            pltpu.VMEM((F, ROWS // F, D), bf16),
            pltpu.VMEM((C, RC, ROWS), bf16),
            pltpu.VMEM((C, F, RC, ROWS), bf16),
            pltpu.VMEM((C, 3 * RC, F * ROWS), bf16),
            pltpu.VMEM((C, F, NB, D), f32),
            pltpu.VMEM((caps, D), bf16),
            pltpu.VMEM((C, F, NB, D + 128), f32),
            pltpu.VMEM((caps, D), bf16),
            pltpu.VMEM((ROWS, D), f32),
            pltpu.VMEM((F, CC, ROWS), bf16),
            pltpu.VMEM((C, F, CC, ROWS), bf16),
            pltpu.VMEM((3 * RC, CC), f32),
            dma((3,)),
            dma((F,)),
            dma((F,)),
            dma((C,)),
            dma((C,)),
            dma((F,)),
            dma((F,)),
            dma((C,)),
            dma((C,)),
            dma((F,)),
            dma((F,)),
            dma((C,)),
            dma((C,)),
            dma((F,)),
            dma((F,)),
            dma((F,)),
            dma((F,)),
            dma((2, half, F)),
            dma((2, half, F)),
        ],
        compiler_params=pltpu.CompilerParams(
            collective_id=0, has_side_effects=True, vmem_limit_bytes=52 * 1024 * 1024
        ),
        cost_estimate=pl.CostEstimate(
            flops=4 * 3 * ROWS * D * D, bytes_accessed=8 * D * D, transcendentals=ROWS * D
        ),
    )(blocks, conv_weight, captions, ids)
    return loss[0, 0], grad_weight, grad_captions


def fits(C, F, frames, captions):
    clip_dev, fr_dev, D = frames.shape
    clips = clip_dev // F
    return (
        C == 8
        and F == 4
        and clips == 8
        and clip_dev % F == 0
        and captions.shape[0] == clips
        and fr_dev * F == FRAMES
        and D % (16 * C) == 0
        and D % 128 == 0
    )


def on_device(frames, conv_weight, captions, positive):
    C, F = lax.axis_size("clip"), lax.axis_size("frame")
    if fits(C, F, frames, captions):
        return fused(C, F, frames, conv_weight, captions, positive)
    return plain(frames, conv_weight, captions, positive)


def solution(mesh):
    placed = (P("clip", "frame", None), P(), P(("clip", "frame"), None), P("clip"))
    return jax.shard_map(
        on_device,
        mesh=mesh,
        in_specs=placed,
        out_specs=(P(), P(None, "clip", "frame"), P(("clip", "frame"), None)),
        check_vma=False,
    )
```

```python
import functools
import math

import jax
import jax.numpy as jnp
from jax import lax
from jax.experimental import pallas as pl
from jax.experimental.pallas import tpu as pltpu
from jax.sharding import PartitionSpec as P

FRAMES = 16


def with_halo(block, sides, width):
    for axis, dim in sides:
        count = lax.axis_size(axis)
        forward = [(i, i + 1) for i in range(count - 1)]
        backward = [(target, source) for source, target in forward]
        low = lax.ppermute(
            lax.slice_in_dim(block, block.shape[dim] - width, None, axis=dim), axis, forward
        )
        high = lax.ppermute(lax.slice_in_dim(block, 0, width, axis=dim), axis, backward)
        block = jnp.concatenate([low, block, high], axis=dim)
    return block


def plain(frames, conv_weight, captions, positive):
    clip_dev, fr_dev, width = frames.shape
    rows = clip_dev * fr_dev
    padded = with_halo(frames, (("frame", 1),), 1)
    shifted = [padded[:, k : k + fr_dev].reshape(rows, width) for k in range(3)]
    conv = jnp.dot(shifted[0], conv_weight[0], preferred_element_type=jnp.float32)
    conv = conv + jnp.dot(shifted[1], conv_weight[1], preferred_element_type=jnp.float32)
    conv = conv + jnp.dot(shifted[2], conv_weight[2], preferred_element_type=jnp.float32)
    hidden = frames.reshape(rows, width).astype(jnp.float32) + jax.nn.gelu(conv)
    partial_pool = jnp.sum(hidden.reshape(clip_dev, fr_dev, width), axis=1)
    pooled = lax.psum(partial_pool, "frame") / FRAMES
    pnorm = jnp.sqrt(jnp.sum(pooled * pooled, axis=1, keepdims=True) + 1e-06)
    unit = pooled / pnorm
    u_low = unit.astype(jnp.bfloat16)
    capf = captions.astype(jnp.float32)
    cnorm = jnp.sqrt(jnp.sum(capf * capf, axis=1, keepdims=True) + 1e-06)
    vunit = capf / cnorm
    v_low = vunit.astype(jnp.bfloat16)
    cap_dev = captions.shape[0]
    frame_pos = lax.axis_index("frame")
    piece = lax.all_gather(v_low, "clip", axis=0, tiled=True)
    count = piece.shape[0]
    place = jnp.arange(count, dtype=jnp.int32)
    ids = place // cap_dev * clip_dev + frame_pos * cap_dev + place % cap_dev
    logits = (
        10.0
        * lax.dot_general(
            u_low, piece, (((1,), (1,)), ((), ())), preferred_element_type=jnp.float32
        )
        - 10.0
    )
    match = (positive[:, None] == ids[None, :]).astype(jnp.float32)
    sign = 2.0 * match - 1.0
    total = jnp.sum(jax.nn.softplus(-sign * logits))
    coef = (10.0 * (jax.nn.sigmoid(logits) - match)).astype(jnp.bfloat16)
    du_acc = jnp.dot(coef, piece, preferred_element_type=jnp.float32)
    dv_piece = lax.dot_general(
        coef, u_low, (((0,), (0,)), ((), ())), preferred_element_type=jnp.float32
    )
    total, du_part, dv_all = (total, du_acc, dv_piece)
    dv_mine = lax.psum_scatter(dv_all, "clip", scatter_dimension=0, tiled=True)
    grad_captions = (dv_mine - vunit * jnp.sum(vunit * dv_mine, axis=1, keepdims=True)) / cnorm
    loss = lax.psum(total, ("clip", "frame")) / (clip_dev * lax.axis_size("clip"))
    du_full = lax.psum(du_part, "frame")
    dpooled = (du_full - unit * jnp.sum(unit * du_full, axis=1, keepdims=True)) / pnorm
    dhidden = jnp.broadcast_to((dpooled / FRAMES)[:, None, :], (clip_dev, fr_dev, width)).reshape(
        rows, width
    )
    _, pull = jax.vjp(jax.nn.gelu, conv)
    dconv = pull(dhidden)[0].astype(jnp.bfloat16).reshape(clip_dev, fr_dev, width)
    dconv_cols = lax.all_to_all(dconv, "frame", split_axis=2, concat_axis=1, tiled=True)
    block = fr_dev + 2
    col_width = dconv_cols.shape[2]
    every_block = lax.all_gather(padded, "frame", axis=1, tiled=True)
    groups = every_block.shape[1] // block
    blocks = every_block.reshape(clip_dev, groups, block, width)
    grads = dconv_cols.reshape(clip_dev, groups, fr_dev, col_width)
    parts = [
        jnp.einsum(
            "cgtd,cgte->de", blocks[:, :, k : k + fr_dev], grads, preferred_element_type=jnp.float32
        )
        for k in range(3)
    ]
    terms = jnp.stack(parts)
    grad_weight = lax.psum_scatter(terms, "clip", scatter_dimension=1, tiled=True)
    return (loss, grad_weight, grad_captions)


MESH = pl.DeviceIdType.MESH


def remote(src, dst, send_sem, recv_sem, device):
    return pltpu.make_async_remote_copy(
        src_ref=src,
        dst_ref=dst,
        send_sem=send_sem,
        recv_sem=recv_sem,
        device_id=device,
        device_id_type=MESH,
    )


def nt_dot(a, b):
    return lax.dot_general(a, b, (((1,), (1,)), ((), ())), preferred_element_type=jnp.float32)


def ring_to_clip(r, count):
    high = r // (count // 2)
    return 2 * r + high * (2 * count - 1 - 4 * r)


def pack(rows, extra):
    cut = (rows.shape[1] + extra.shape[1]) // 2
    bottom = jnp.concatenate([rows[:, cut:], extra], axis=1)
    return jnp.concatenate([rows[:, :cut], bottom], axis=0).astype(jnp.bfloat16)


def unpack(units, width):
    C, F, tall, cut = units.shape
    flat = units.reshape(C * F, tall, cut).astype(jnp.float32)
    top = flat[:, : tall // 2].reshape(C * F * tall // 2, cut)
    bottom = flat[:, tall // 2 :].reshape(C * F * tall // 2, cut)
    rows = jnp.concatenate([top, bottom[:, : width - cut]], axis=1)
    return rows.astype(jnp.bfloat16), bottom[:, width - cut :]


def fused_kernel(
    C,
    F,
    frames_ref,
    w_hbm,
    cap_ref,
    pos_ref,
    split_ref,
    loss_ref,
    gw_ref,
    gc_ref,
    w_ref,
    x_rows,
    xt,
    xu,
    x3,
    vu,
    vb,
    uu,
    ub,
    slope,
    dt,
    dbuf,
    acc,
    w_sem,
    fr_send,
    fr_recv,
    v1_send,
    v1_recv,
    v2_send,
    v2_recv,
    x1_send,
    x1_recv,
    x2_send,
    x2_recv,
    u1_send,
    u1_recv,
    u2_send,
    u2_recv,
    da_send,
    da_recv,
    ring_send,
    ring_recv,
):
    D = cap_ref.shape[1]
    NB = cap_ref.shape[0]
    T = FRAMES
    ROWS = T * NB
    part = ROWS // F
    RC = D // C
    CC = D // F
    c = lax.axis_index("clip")
    f = lax.axis_index("frame")
    half = C // 2
    z = c // 2
    pos = z + (c - 2 * z) * (C - 1 - 2 * z)
    right = ring_to_clip(lax.rem(pos + 1, C), C)
    left = ring_to_clip(lax.rem(pos + C - 1, C), C)

    w_copies = [pltpu.make_async_copy(w_hbm.at[k], w_ref.at[k], w_sem.at[k]) for k in range(3)]
    for copy in w_copies:
        copy.start()

    def cpeer(d):
        return lax.rem(c + d, C)

    def fpeer(d):
        return lax.rem(f + d, F)

    barrier = pltpu.get_barrier_semaphore()
    for d in range(1, C):
        pl.semaphore_signal(barrier, inc=1, device_id=(cpeer(d), f), device_id_type=MESH)
    for d in range(1, F):
        pl.semaphore_signal(barrier, inc=1, device_id=(c, fpeer(d)), device_id_type=MESH)
    pl.semaphore_wait(barrier, C + F - 2)

    sends = []

    def go(copy):
        copy.start()
        sends.append(copy)

    across = lax.rem(f + F // 2, F)
    beside = f + 1 - 2 * lax.rem(f, 2)
    diagonal = lax.rem(beside + F // 2, F)

    def spread(array, send_sem, recv_sem):
        slab = array.at[:, f]
        go(remote(slab, slab, send_sem.at[0], recv_sem.at[0], (c, across)))
        go(remote(slab, slab, send_sem.at[1], recv_sem.at[1], (c, beside)))

    def spread_on(array, send_sem, recv_sem):
        slab = array.at[:, across]
        remote(slab, slab, send_sem.at[0], recv_sem.at[0], (c, across)).wait_recv()
        go(remote(slab, slab, send_sem.at[2], recv_sem.at[2], (c, beside)))

    def spread_end(array, send_sem, recv_sem):
        for i, source in ((1, beside), (2, diagonal)):
            slab = array.at[:, source]
            remote(slab, slab, send_sem.at[i], recv_sem.at[i], (c, beside)).wait_recv()

    def clip_arrive(array, send_sem, recv_sem):
        for d in range(1, C):
            source = cpeer(C - d)
            slot = array.at[source, f]
            remote(slot, slot, send_sem.at[d], recv_sem.at[d], (source, f)).wait_recv()

    for d in range(1, F):
        go(
            remote(
                frames_ref.at[fpeer(d)],
                x_rows.at[f],
                fr_send.at[d],
                fr_recv.at[d],
                (c, fpeer(d)),
            )
        )
    x_rows[f] = frames_ref[f]

    capf = cap_ref[...].astype(jnp.float32)
    cnorm = jnp.sqrt(jnp.sum(capf * capf, axis=1, keepdims=True) + 1e-06)
    vunit = capf / cnorm
    v_own = vunit.astype(jnp.bfloat16)
    vu[c, f] = pack(v_own.astype(jnp.float32), jnp.zeros((NB, 128), jnp.float32))
    for d in range(1, C):
        go(remote(vu.at[c, f], vu.at[c, f], v1_send.at[d], v1_recv.at[d], (cpeer(d), f)))

    for d in range(1, F):
        source = fpeer(F - d)
        remote(
            x_rows.at[source], x_rows.at[source], fr_send.at[d], fr_recv.at[d], (c, source)
        ).wait_recv()
    xf = x_rows[...].reshape(ROWS, D).astype(jnp.float32)
    xt[...] = xf.T.astype(jnp.bfloat16).reshape(C, RC, ROWS)
    for d in range(1, C):
        to = cpeer(d)
        go(remote(xt.at[to], xu.at[c, f], x1_send.at[d], x1_recv.at[d], (to, f)))
    xu[c, f] = xt[c]

    edge = jnp.zeros((NB, D), jnp.float32)
    before = jnp.concatenate([edge, xf[: ROWS - NB]], axis=0).astype(jnp.bfloat16)
    after = jnp.concatenate([xf[NB:], edge], axis=0).astype(jnp.bfloat16)
    w_copies[0].wait()
    conv = jnp.dot(before, w_ref[0], preferred_element_type=jnp.float32)

    clip_arrive(vu, v1_send, v1_recv)
    spread(vu, v2_send, v2_recv)

    w_copies[1].wait()
    conv = conv + jnp.dot(
        x_rows[...].reshape(ROWS, D), w_ref[1], preferred_element_type=jnp.float32
    )
    clip_arrive(xu, x1_send, x1_recv)
    spread(xu, x2_send, x2_recv)
    w_copies[2].wait()
    conv = conv + jnp.dot(after, w_ref[2], preferred_element_type=jnp.float32)

    spread_on(vu, v2_send, v2_recv)

    scale = math.sqrt(2.0 / math.pi)
    square = conv * conv
    tanh = jnp.tanh(scale * conv * (1.0 + 0.044715 * square))
    cdf = 0.5 * (1.0 + tanh)
    slope[...] = cdf + (0.5 * scale) * conv * (1.0 - tanh * tanh) * (1.0 + 0.134145 * square)
    hidden = xf + conv * cdf
    pooled = jnp.sum(hidden.reshape(T, NB, D), axis=0) * (1.0 / T)
    pnorm = jnp.sqrt(jnp.sum(pooled * pooled, axis=1, keepdims=True) + 1e-06)
    unit = pooled / pnorm
    u_low = unit.astype(jnp.bfloat16)
    pos_own = pos_ref[f]
    uu[c, f] = pack(u_low.astype(jnp.float32), split_ref[f])
    for d in range(1, C):
        go(remote(uu.at[c, f], uu.at[c, f], u1_send.at[d], u1_recv.at[d], (cpeer(d), f)))

    spread_end(vu, v2_send, v2_recv)
    caps = C * F * NB
    vb[...] = unpack(vu[...], D)[0]
    logits = 10.0 * nt_dot(u_low, vb[...]) - 10.0
    ids = lax.broadcasted_iota(jnp.int32, (NB, caps), 1).astype(jnp.float32)
    match = jnp.where(pos_own[:, :1] == ids, 1.0, 0.0)
    coef = (10.0 * (1.0 / (1.0 + jnp.exp(-logits)) - match)).astype(jnp.bfloat16)
    du = jnp.dot(coef, vb[...], preferred_element_type=jnp.float32)
    dpooled = (du - unit * jnp.sum(unit * du, axis=1, keepdims=True)) / pnorm
    step = dpooled * (1.0 / T)
    dconv = (slope[...].reshape(T, NB, D) * step[None]).reshape(ROWS, D)
    dt[...] = dconv.T.astype(jnp.bfloat16).reshape(F, CC, ROWS)
    for d in range(1, F):
        to = fpeer(d)
        go(remote(dt.at[to], dbuf.at[c, f], da_send.at[d], da_recv.at[d], (c, to)))
    dbuf[c, f] = dt[f]

    ways = (right, left)

    def block_at(way, hop):
        return ring_to_clip(lax.rem(pos + (C - hop if way == 0 else hop), C), C)

    def units_at(way, hop):
        if hop < half:
            return range(F)
        return range(F // 2) if way == 0 else range(F // 2, F)

    def forward(way, hop, q):
        slot = dbuf.at[block_at(way, hop), fpeer(F - q)]
        go(
            remote(
                slot,
                slot,
                ring_send.at[way, hop, q],
                ring_recv.at[way, hop, q],
                (ways[way], f),
            )
        )

    def arrive(way, hop, q):
        slot = dbuf.at[block_at(way, hop), fpeer(F - q)]
        remote(
            slot,
            slot,
            ring_send.at[way, hop - 1, q],
            ring_recv.at[way, hop - 1, q],
            (ways[way], f),
        ).wait_recv()

    def relay(hop):
        for q in range(F):
            for way in range(2):
                if q in units_at(way, hop):
                    arrive(way, hop, q)
                    if hop < half and q in units_at(way, hop + 1):
                        forward(way, hop, q)

    def add_block(block, first=False):
        rhs = jnp.concatenate([dbuf[block, i] for i in range(F)], axis=1)
        term = nt_dot(x3[block], rhs)
        if first:
            acc[...] = term
        else:
            acc[...] += term

    for q in range(F):
        if q:
            source = fpeer(F - q)
            slot = dbuf.at[c, source]
            remote(slot, slot, da_send.at[q], da_recv.at[q], (c, source)).wait_recv()
        for way in range(2):
            if q in units_at(way, 1):
                forward(way, 0, q)

    spread_on(xu, x2_send, x2_recv)
    spread_end(xu, x2_send, x2_recv)
    row = lax.broadcasted_iota(jnp.int32, (ROWS, ROWS), 0)
    col = lax.broadcasted_iota(jnp.int32, (ROWS, ROWS), 1)
    later = jnp.where(row == col - NB, 1.0, 0.0)
    earlier = jnp.where(row == col + NB, 1.0, 0.0)
    moves = jnp.concatenate([later, earlier], axis=1).astype(jnp.bfloat16)

    def shift(block, carry):
        units = xu[block]
        moved = jnp.dot(
            units.reshape(F * RC, ROWS), moves, preferred_element_type=jnp.float32
        ).astype(jnp.bfloat16)
        for i in range(F):
            lanes = slice(i * ROWS, (i + 1) * ROWS)
            rows = slice(i * RC, (i + 1) * RC)
            x3[block, 0:RC, lanes] = moved[rows, :ROWS]
            x3[block, RC : 2 * RC, lanes] = units[i]
            x3[block, 2 * RC :, lanes] = moved[rows, ROWS:]
        return carry

    lax.fori_loop(0, C, shift, 0)
    add_block(c, first=True)

    relay(1)
    clip_arrive(uu, u1_send, u1_recv)
    spread(uu, u2_send, u2_recv)
    add_block(block_at(0, 1))
    add_block(block_at(1, 1))

    relay(2)
    spread_on(uu, u2_send, u2_recv)
    add_block(block_at(0, 2))
    add_block(block_at(1, 2))

    relay(3)

    spread_end(uu, u2_send, u2_recv)
    u_all, halves = unpack(uu[...], D)
    ub[...] = u_all
    pos_all = 128.0 * halves[:, :1] + halves[:, 64:65]
    turned = halves.T
    pos_row = 128.0 * turned[:1] + turned[64:65]
    first_id = (c * F + f) * NB
    own_ids = (first_id + lax.broadcasted_iota(jnp.int32, (NB, caps), 0)).astype(jnp.float32)
    match_own = jnp.where(pos_row == own_ids, 1.0, 0.0)
    logits_own = 10.0 * nt_dot(v_own, ub[...]) - 10.0
    coef_own = (10.0 * (1.0 / (1.0 + jnp.exp(-logits_own)) - match_own)).astype(jnp.bfloat16)
    dv = jnp.dot(coef_own, ub[...], preferred_element_type=jnp.float32)
    gc_ref[...] = (dv - vunit * jnp.sum(vunit * dv, axis=1, keepdims=True)) / cnorm

    every = 10.0 * nt_dot(ub[...], vb[...]) - 10.0
    all_ids = lax.broadcasted_iota(jnp.int32, (caps, caps), 1).astype(jnp.float32)
    signed = jnp.where(pos_all == all_ids, -every, every)
    soft = jnp.maximum(signed, 0.0) + jnp.log1p(jnp.exp(-jnp.abs(signed)))
    total = jnp.sum(jnp.sum(soft, axis=0, keepdims=True), axis=1, keepdims=True)
    loss_ref[...] = jnp.broadcast_to(total * (1.0 / caps), loss_ref.shape)

    add_block(block_at(0, 3))
    add_block(block_at(1, 3))
    relay(4)
    add_block(block_at(0, 4))
    gw_ref[...] = acc[...].reshape(3, RC, CC)
    for copy in sends:
        copy.wait_send()


def fused(C, F, frames, conv_weight, captions, positive):
    clip_dev, fr_dev, D = frames.shape
    NB = clip_dev // F
    ROWS = FRAMES * NB
    RC, CC = D // C, D // F
    half = C // 2
    blocks = frames.reshape(F, NB, fr_dev, D).transpose(0, 2, 1, 3).reshape(F, fr_dev * NB, D)
    ids = jnp.broadcast_to(positive.reshape(F, NB, 1), (F, NB, 128))
    split = jnp.where(jnp.arange(128) < 64, ids // 128, ids % 128).astype(jnp.float32)
    ids = ids.astype(jnp.float32)
    vmem = pl.BlockSpec(memory_space=pltpu.VMEM)
    dma = pltpu.SemaphoreType.DMA
    bf16, f32 = jnp.bfloat16, jnp.float32
    caps = C * F * NB
    loss, grad_weight, grad_captions = pl.pallas_call(
        functools.partial(fused_kernel, C, F),
        out_shape=(
            jax.ShapeDtypeStruct((8, 128), f32),
            jax.ShapeDtypeStruct((3, RC, CC), f32),
            jax.ShapeDtypeStruct((NB, D), f32),
        ),
        in_specs=[vmem, pl.BlockSpec(memory_space=pl.ANY), vmem, vmem, vmem],
        out_specs=(vmem, vmem, vmem),
        scratch_shapes=[
            pltpu.VMEM((3, D, D), bf16),
            pltpu.VMEM((F, ROWS // F, D), bf16),
            pltpu.VMEM((C, RC, ROWS), bf16),
            pltpu.VMEM((C, F, RC, ROWS), bf16),
            pltpu.VMEM((C, 3 * RC, F * ROWS), bf16),
            pltpu.VMEM((C, F, 2 * NB, (D + 128) // 2), bf16),
            pltpu.VMEM((caps, D), bf16),
            pltpu.VMEM((C, F, 2 * NB, (D + 128) // 2), bf16),
            pltpu.VMEM((caps, D), bf16),
            pltpu.VMEM((ROWS, D), f32),
            pltpu.VMEM((F, CC, ROWS), bf16),
            pltpu.VMEM((C, F, CC, ROWS), bf16),
            pltpu.VMEM((3 * RC, CC), f32),
            dma((3,)),
            dma((F,)),
            dma((F,)),
            dma((C,)),
            dma((C,)),
            dma((F,)),
            dma((F,)),
            dma((C,)),
            dma((C,)),
            dma((F,)),
            dma((F,)),
            dma((C,)),
            dma((C,)),
            dma((F,)),
            dma((F,)),
            dma((F,)),
            dma((F,)),
            dma((2, half, F)),
            dma((2, half, F)),
        ],
        compiler_params=pltpu.CompilerParams(
            collective_id=0, has_side_effects=True, vmem_limit_bytes=52 * 1024 * 1024
        ),
        cost_estimate=pl.CostEstimate(
            flops=4 * 3 * ROWS * D * D, bytes_accessed=8 * D * D, transcendentals=ROWS * D
        ),
    )(blocks, conv_weight, captions, ids, split)
    return loss[0, 0], grad_weight, grad_captions


def fits(C, F, frames, captions):
    clip_dev, fr_dev, D = frames.shape
    clips = clip_dev // F
    return (
        C == 8
        and F == 4
        and clips == 8
        and clip_dev % F == 0
        and captions.shape[0] == clips
        and fr_dev * F == FRAMES
        and D % (16 * C) == 0
        and D % 128 == 0
    )


def on_device(frames, conv_weight, captions, positive):
    C, F = lax.axis_size("clip"), lax.axis_size("frame")
    if fits(C, F, frames, captions):
        return fused(C, F, frames, conv_weight, captions, positive)
    return plain(frames, conv_weight, captions, positive)


def solution(mesh):
    placed = (P("clip", "frame", None), P(), P(("clip", "frame"), None), P("clip"))
    return jax.shard_map(
        on_device,
        mesh=mesh,
        in_specs=placed,
        out_specs=(P(), P(None, "clip", "frame"), P(("clip", "frame"), None)),
        check_vma=False,
    )
```

```python
import functools
import math

import jax
import jax.numpy as jnp
from jax import lax
from jax.experimental import pallas as pl
from jax.experimental.pallas import tpu as pltpu
from jax.sharding import PartitionSpec as P

FRAMES = 16


def with_halo(block, sides, width):
    for axis, dim in sides:
        count = lax.axis_size(axis)
        forward = [(i, i + 1) for i in range(count - 1)]
        backward = [(target, source) for source, target in forward]
        low = lax.ppermute(
            lax.slice_in_dim(block, block.shape[dim] - width, None, axis=dim), axis, forward
        )
        high = lax.ppermute(lax.slice_in_dim(block, 0, width, axis=dim), axis, backward)
        block = jnp.concatenate([low, block, high], axis=dim)
    return block


def plain(frames, conv_weight, captions, positive):
    clip_dev, fr_dev, width = frames.shape
    rows = clip_dev * fr_dev
    padded = with_halo(frames, (("frame", 1),), 1)
    shifted = [padded[:, k : k + fr_dev].reshape(rows, width) for k in range(3)]
    conv = jnp.dot(shifted[0], conv_weight[0], preferred_element_type=jnp.float32)
    conv = conv + jnp.dot(shifted[1], conv_weight[1], preferred_element_type=jnp.float32)
    conv = conv + jnp.dot(shifted[2], conv_weight[2], preferred_element_type=jnp.float32)
    hidden = frames.reshape(rows, width).astype(jnp.float32) + jax.nn.gelu(conv)
    partial_pool = jnp.sum(hidden.reshape(clip_dev, fr_dev, width), axis=1)
    pooled = lax.psum(partial_pool, "frame") / FRAMES
    pnorm = jnp.sqrt(jnp.sum(pooled * pooled, axis=1, keepdims=True) + 1e-06)
    unit = pooled / pnorm
    u_low = unit.astype(jnp.bfloat16)
    capf = captions.astype(jnp.float32)
    cnorm = jnp.sqrt(jnp.sum(capf * capf, axis=1, keepdims=True) + 1e-06)
    vunit = capf / cnorm
    v_low = vunit.astype(jnp.bfloat16)
    cap_dev = captions.shape[0]
    frame_pos = lax.axis_index("frame")
    piece = lax.all_gather(v_low, "clip", axis=0, tiled=True)
    count = piece.shape[0]
    place = jnp.arange(count, dtype=jnp.int32)
    ids = place // cap_dev * clip_dev + frame_pos * cap_dev + place % cap_dev
    logits = (
        10.0
        * lax.dot_general(
            u_low, piece, (((1,), (1,)), ((), ())), preferred_element_type=jnp.float32
        )
        - 10.0
    )
    match = (positive[:, None] == ids[None, :]).astype(jnp.float32)
    sign = 2.0 * match - 1.0
    total = jnp.sum(jax.nn.softplus(-sign * logits))
    coef = (10.0 * (jax.nn.sigmoid(logits) - match)).astype(jnp.bfloat16)
    du_acc = jnp.dot(coef, piece, preferred_element_type=jnp.float32)
    dv_piece = lax.dot_general(
        coef, u_low, (((0,), (0,)), ((), ())), preferred_element_type=jnp.float32
    )
    total, du_part, dv_all = (total, du_acc, dv_piece)
    dv_mine = lax.psum_scatter(dv_all, "clip", scatter_dimension=0, tiled=True)
    grad_captions = (dv_mine - vunit * jnp.sum(vunit * dv_mine, axis=1, keepdims=True)) / cnorm
    loss = lax.psum(total, ("clip", "frame")) / (clip_dev * lax.axis_size("clip"))
    du_full = lax.psum(du_part, "frame")
    dpooled = (du_full - unit * jnp.sum(unit * du_full, axis=1, keepdims=True)) / pnorm
    dhidden = jnp.broadcast_to((dpooled / FRAMES)[:, None, :], (clip_dev, fr_dev, width)).reshape(
        rows, width
    )
    _, pull = jax.vjp(jax.nn.gelu, conv)
    dconv = pull(dhidden)[0].astype(jnp.bfloat16).reshape(clip_dev, fr_dev, width)
    dconv_cols = lax.all_to_all(dconv, "frame", split_axis=2, concat_axis=1, tiled=True)
    block = fr_dev + 2
    col_width = dconv_cols.shape[2]
    every_block = lax.all_gather(padded, "frame", axis=1, tiled=True)
    groups = every_block.shape[1] // block
    blocks = every_block.reshape(clip_dev, groups, block, width)
    grads = dconv_cols.reshape(clip_dev, groups, fr_dev, col_width)
    parts = [
        jnp.einsum(
            "cgtd,cgte->de", blocks[:, :, k : k + fr_dev], grads, preferred_element_type=jnp.float32
        )
        for k in range(3)
    ]
    terms = jnp.stack(parts)
    grad_weight = lax.psum_scatter(terms, "clip", scatter_dimension=1, tiled=True)
    return (loss, grad_weight, grad_captions)


MESH = pl.DeviceIdType.MESH


def remote(src, dst, send_sem, recv_sem, device):
    return pltpu.make_async_remote_copy(
        src_ref=src,
        dst_ref=dst,
        send_sem=send_sem,
        recv_sem=recv_sem,
        device_id=device,
        device_id_type=MESH,
    )


def nt_dot(a, b):
    return lax.dot_general(a, b, (((1,), (1,)), ((), ())), preferred_element_type=jnp.float32)


def ring_to_clip(r, count):
    high = r // (count // 2)
    return 2 * r + high * (2 * count - 1 - 4 * r)


def pack(rows, extra):
    cut = (rows.shape[1] + extra.shape[1]) // 2
    bottom = jnp.concatenate([rows[:, cut:], extra], axis=1)
    return jnp.concatenate([rows[:, :cut], bottom], axis=0).astype(jnp.bfloat16)


def unpack(units, width):
    C, F, tall, cut = units.shape
    flat = units.reshape(C * F, tall, cut).astype(jnp.float32)
    top = flat[:, : tall // 2].reshape(C * F * tall // 2, cut)
    bottom = flat[:, tall // 2 :].reshape(C * F * tall // 2, cut)
    rows = jnp.concatenate([top, bottom[:, : width - cut]], axis=1)
    return rows.astype(jnp.bfloat16), bottom[:, width - cut :]


def fused_kernel(
    C,
    F,
    frames_ref,
    w_hbm,
    cap_hbm,
    pos_hbm,
    loss_ref,
    gw_ref,
    gc_ref,
    cap_ref,
    pos_ref,
    w_ref,
    x_rows,
    xt,
    xu,
    x3,
    vu,
    vb,
    uu,
    ub,
    slope,
    dt,
    dbuf,
    acc,
    cap_sem,
    pos_sem,
    w_sem,
    fr_send,
    fr_recv,
    v1_send,
    v1_recv,
    v2_send,
    v2_recv,
    x1_send,
    x1_recv,
    x2_send,
    x2_recv,
    u1_send,
    u1_recv,
    u2_send,
    u2_recv,
    da_send,
    da_recv,
    ring_send,
    ring_recv,
):
    D = cap_ref.shape[1]
    NB = cap_ref.shape[0]
    T = FRAMES
    ROWS = T * NB
    part = ROWS // F
    RC = D // C
    CC = D // F
    c = lax.axis_index("clip")
    f = lax.axis_index("frame")
    half = C // 2
    z = c // 2
    pos = z + (c - 2 * z) * (C - 1 - 2 * z)
    right = ring_to_clip(lax.rem(pos + 1, C), C)
    left = ring_to_clip(lax.rem(pos + C - 1, C), C)

    cap_copy = pltpu.make_async_copy(cap_hbm, cap_ref, cap_sem)
    cap_copy.start()
    pos_copy = pltpu.make_async_copy(pos_hbm, pos_ref, pos_sem)
    pos_copy.start()
    w_copies = [pltpu.make_async_copy(w_hbm.at[k], w_ref.at[k], w_sem.at[k]) for k in range(3)]
    for copy in w_copies:
        copy.start()

    def cpeer(d):
        return lax.rem(c + d, C)

    def fpeer(d):
        return lax.rem(f + d, F)

    barrier = pltpu.get_barrier_semaphore()
    for d in range(1, C):
        pl.semaphore_signal(barrier, inc=1, device_id=(cpeer(d), f), device_id_type=MESH)
    for d in range(1, F):
        pl.semaphore_signal(barrier, inc=1, device_id=(c, fpeer(d)), device_id_type=MESH)
    pl.semaphore_wait(barrier, C + F - 2)

    sends = []

    def go(copy):
        copy.start()
        sends.append(copy)

    across = lax.rem(f + F // 2, F)
    beside = f + 1 - 2 * lax.rem(f, 2)
    diagonal = lax.rem(beside + F // 2, F)

    def spread(array, send_sem, recv_sem):
        slab = array.at[:, f]
        go(remote(slab, slab, send_sem.at[0], recv_sem.at[0], (c, across)))
        go(remote(slab, slab, send_sem.at[1], recv_sem.at[1], (c, beside)))

    def spread_on(array, send_sem, recv_sem):
        slab = array.at[:, across]
        remote(slab, slab, send_sem.at[0], recv_sem.at[0], (c, across)).wait_recv()
        go(remote(slab, slab, send_sem.at[2], recv_sem.at[2], (c, beside)))

    def spread_end(array, send_sem, recv_sem):
        for i, source in ((1, beside), (2, diagonal)):
            slab = array.at[:, source]
            remote(slab, slab, send_sem.at[i], recv_sem.at[i], (c, beside)).wait_recv()

    def clip_arrive(array, send_sem, recv_sem):
        for d in range(1, C):
            source = cpeer(C - d)
            slot = array.at[source, f]
            remote(slot, slot, send_sem.at[d], recv_sem.at[d], (source, f)).wait_recv()

    for d in range(1, F):
        go(
            remote(
                frames_ref.at[fpeer(d)],
                x_rows.at[f],
                fr_send.at[d],
                fr_recv.at[d],
                (c, fpeer(d)),
            )
        )
    x_rows[f] = frames_ref[f]

    cap_copy.wait()
    pos_copy.wait()
    capf = cap_ref[...].astype(jnp.float32)
    cnorm = jnp.sqrt(jnp.sum(capf * capf, axis=1, keepdims=True) + 1e-06)
    vunit = capf / cnorm
    v_own = vunit.astype(jnp.bfloat16)
    vu[c, f] = pack(v_own.astype(jnp.float32), jnp.zeros((NB, 128), jnp.float32))
    for d in range(1, C):
        go(remote(vu.at[c, f], vu.at[c, f], v1_send.at[d], v1_recv.at[d], (cpeer(d), f)))

    for d in range(1, F):
        source = fpeer(F - d)
        remote(
            x_rows.at[source], x_rows.at[source], fr_send.at[d], fr_recv.at[d], (c, source)
        ).wait_recv()
    xf = x_rows[...].reshape(ROWS, D).astype(jnp.float32)
    edge = jnp.zeros((NB, D), jnp.float32)
    before = jnp.concatenate([edge, xf[: ROWS - NB]], axis=0).astype(jnp.bfloat16)
    after = jnp.concatenate([xf[NB:], edge], axis=0).astype(jnp.bfloat16)
    w_copies[0].wait()
    conv = jnp.dot(before, w_ref[0], preferred_element_type=jnp.float32)
    xt[...] = xf.T.astype(jnp.bfloat16).reshape(C, RC, ROWS)
    for d in range(1, C):
        to = cpeer(d)
        go(remote(xt.at[to], xu.at[c, f], x1_send.at[d], x1_recv.at[d], (to, f)))
    xu[c, f] = xt[c]

    clip_arrive(vu, v1_send, v1_recv)
    spread(vu, v2_send, v2_recv)

    w_copies[1].wait()
    conv = conv + jnp.dot(
        x_rows[...].reshape(ROWS, D), w_ref[1], preferred_element_type=jnp.float32
    )
    w_copies[2].wait()
    conv = conv + jnp.dot(after, w_ref[2], preferred_element_type=jnp.float32)

    spread_on(vu, v2_send, v2_recv)

    scale = math.sqrt(2.0 / math.pi)
    square = conv * conv
    tanh = jnp.tanh(scale * conv * (1.0 + 0.044715 * square))
    cdf = 0.5 * (1.0 + tanh)
    slope[...] = cdf + (0.5 * scale) * conv * (1.0 - tanh * tanh) * (1.0 + 0.134145 * square)
    hidden = xf + conv * cdf
    pooled = jnp.sum(hidden.reshape(T, NB, D), axis=0) * (1.0 / T)
    pnorm = jnp.sqrt(jnp.sum(pooled * pooled, axis=1, keepdims=True) + 1e-06)
    unit = pooled / pnorm
    u_low = unit.astype(jnp.bfloat16)
    lanes = lax.broadcasted_iota(jnp.int32, (NB, F * NB), 1)
    mine = lanes == f * NB + lax.broadcasted_iota(jnp.int32, (NB, F * NB), 0)
    every_pos = jnp.broadcast_to(pos_ref[...].astype(jnp.float32), (NB, F * NB))
    pos_own = jnp.sum(jnp.where(mine, every_pos, 0.0), axis=1, keepdims=True)
    high = jnp.floor(pos_own * (1.0 / 128.0))
    lane = lax.broadcasted_iota(jnp.int32, (NB, 128), 1)
    split = jnp.where(lane < 64, high, pos_own - 128.0 * high)
    uu[c, f] = pack(u_low.astype(jnp.float32), split)
    for d in range(1, C):
        go(remote(uu.at[c, f], uu.at[c, f], u1_send.at[d], u1_recv.at[d], (cpeer(d), f)))

    clip_arrive(xu, x1_send, x1_recv)
    spread(xu, x2_send, x2_recv)

    spread_end(vu, v2_send, v2_recv)
    caps = C * F * NB
    vb[...] = unpack(vu[...], D)[0]
    logits = 10.0 * nt_dot(u_low, vb[...]) - 10.0
    ids = lax.broadcasted_iota(jnp.int32, (NB, caps), 1).astype(jnp.float32)
    match = jnp.where(pos_own == ids, 1.0, 0.0)
    coef = (10.0 * (1.0 / (1.0 + jnp.exp(-logits)) - match)).astype(jnp.bfloat16)
    du = jnp.dot(coef, vb[...], preferred_element_type=jnp.float32)
    dpooled = (du - unit * jnp.sum(unit * du, axis=1, keepdims=True)) / pnorm
    step = dpooled * (1.0 / T)
    dconv = (slope[...].reshape(T, NB, D) * step[None]).reshape(ROWS, D)
    dt[...] = dconv.T.astype(jnp.bfloat16).reshape(F, CC, ROWS)
    for d in range(1, F):
        to = fpeer(d)
        go(remote(dt.at[to], dbuf.at[c, f], da_send.at[d], da_recv.at[d], (c, to)))
    dbuf[c, f] = dt[f]

    ways = (right, left)

    def block_at(way, hop):
        return ring_to_clip(lax.rem(pos + (C - hop if way == 0 else hop), C), C)

    def units_at(way, hop):
        if hop < half:
            return range(F)
        return range(F // 2) if way == 0 else range(F // 2, F)

    def forward(way, hop, q):
        slot = dbuf.at[block_at(way, hop), fpeer(F - q)]
        go(
            remote(
                slot,
                slot,
                ring_send.at[way, hop, q],
                ring_recv.at[way, hop, q],
                (ways[way], f),
            )
        )

    def arrive(way, hop, q):
        slot = dbuf.at[block_at(way, hop), fpeer(F - q)]
        remote(
            slot,
            slot,
            ring_send.at[way, hop - 1, q],
            ring_recv.at[way, hop - 1, q],
            (ways[way], f),
        ).wait_recv()

    def relay(hop, *which):
        for q in which:
            for way in range(2):
                if q in units_at(way, hop):
                    arrive(way, hop, q)
                    if hop < half and q in units_at(way, hop + 1):
                        forward(way, hop, q)

    def block_term(block):
        rhs = jnp.concatenate([dbuf[block, i] for i in range(F)], axis=1)
        return nt_dot(x3[block], rhs)

    def add_block(block, first=False):
        if first:
            acc[...] = block_term(block)
        else:
            acc[...] += block_term(block)

    for q in range(F):
        if q:
            source = fpeer(F - q)
            slot = dbuf.at[c, source]
            remote(slot, slot, da_send.at[q], da_recv.at[q], (c, source)).wait_recv()
        for way in range(2):
            if q in units_at(way, 1):
                forward(way, 0, q)

    relay(1, 0)
    spread_on(xu, x2_send, x2_recv)
    spread_end(xu, x2_send, x2_recv)
    row = lax.broadcasted_iota(jnp.int32, (ROWS, ROWS), 0)
    col = lax.broadcasted_iota(jnp.int32, (ROWS, ROWS), 1)
    later = jnp.where(row == col - NB, 1.0, 0.0)
    earlier = jnp.where(row == col + NB, 1.0, 0.0)
    moves = jnp.concatenate([later, earlier], axis=1).astype(jnp.bfloat16)

    def shift(block, carry):
        units = xu[block]
        moved = jnp.dot(
            units.reshape(F * RC, ROWS), moves, preferred_element_type=jnp.float32
        ).astype(jnp.bfloat16)
        for i in range(F):
            lanes = slice(i * ROWS, (i + 1) * ROWS)
            rows = slice(i * RC, (i + 1) * RC)
            x3[block, 0:RC, lanes] = moved[rows, :ROWS]
            x3[block, RC : 2 * RC, lanes] = units[i]
            x3[block, 2 * RC :, lanes] = moved[rows, ROWS:]
        return carry

    quarter = C // 4
    lax.fori_loop(0, quarter, shift, 0)
    relay(1, 1)
    lax.fori_loop(quarter, 2 * quarter, shift, 0)
    relay(1, 2)
    lax.fori_loop(2 * quarter, 3 * quarter, shift, 0)
    relay(1, 3)
    clip_arrive(uu, u1_send, u1_recv)
    spread(uu, u2_send, u2_recv)
    lax.fori_loop(3 * quarter, C, shift, 0)
    relay(2, 0)
    add_block(c, first=True)
    relay(2, 1)
    add_block(block_at(0, 1))
    relay(2, 2)
    add_block(block_at(1, 1))
    relay(2, 3)
    spread_on(uu, u2_send, u2_recv)
    relay(3, 0)
    add_block(block_at(0, 2))
    relay(3, 1)
    add_block(block_at(1, 2))
    relay(3, 2)
    spread_end(uu, u2_send, u2_recv)
    u_all, halves = unpack(uu[...], D)
    ub[...] = u_all
    pos_all = 128.0 * halves[:, :1] + halves[:, 64:65]
    turned = halves.T
    pos_row = 128.0 * turned[:1] + turned[64:65]
    first_id = (c * F + f) * NB
    own_ids = (first_id + lax.broadcasted_iota(jnp.int32, (NB, caps), 0)).astype(jnp.float32)
    match_own = jnp.where(pos_row == own_ids, 1.0, 0.0)
    logits_own = 10.0 * nt_dot(v_own, ub[...]) - 10.0
    coef_own = (10.0 * (1.0 / (1.0 + jnp.exp(-logits_own)) - match_own)).astype(jnp.bfloat16)
    dv = jnp.dot(coef_own, ub[...], preferred_element_type=jnp.float32)
    gc_ref[...] = (dv - vunit * jnp.sum(vunit * dv, axis=1, keepdims=True)) / cnorm

    relay(3, 3)
    every = 10.0 * nt_dot(ub[...], vb[...]) - 10.0
    all_ids = lax.broadcasted_iota(jnp.int32, (caps, caps), 1).astype(jnp.float32)
    signed = jnp.where(pos_all == all_ids, -every, every)
    soft = jnp.maximum(signed, 0.0) + jnp.log1p(jnp.exp(-jnp.abs(signed)))
    total = jnp.sum(jnp.sum(soft, axis=0, keepdims=True), axis=1, keepdims=True)
    loss_ref[...] = jnp.broadcast_to(total * (1.0 / caps), loss_ref.shape)

    add_block(block_at(0, 3))
    add_block(block_at(1, 3))
    relay(4, *range(F))
    gw_ref[...] = (acc[...] + block_term(block_at(0, 4))).reshape(3, RC, CC)
    for copy in sends:
        copy.wait_send()


def fused(C, F, frames, conv_weight, captions, positive):
    clip_dev, fr_dev, D = frames.shape
    NB = clip_dev // F
    ROWS = FRAMES * NB
    RC, CC = D // C, D // F
    half = C // 2
    blocks = frames.reshape(F, NB, fr_dev, D).transpose(0, 2, 1, 3).reshape(F, fr_dev * NB, D)
    vmem = pl.BlockSpec(memory_space=pltpu.VMEM)
    hbm = pl.BlockSpec(memory_space=pltpu.HBM)
    dma = pltpu.SemaphoreType.DMA
    bf16, f32 = jnp.bfloat16, jnp.float32
    caps = C * F * NB
    loss, grad_weight, grad_captions = pl.pallas_call(
        functools.partial(fused_kernel, C, F),
        out_shape=(
            jax.ShapeDtypeStruct((8, 128), f32),
            jax.ShapeDtypeStruct((3, RC, CC), f32),
            jax.ShapeDtypeStruct((NB, D), f32),
        ),
        in_specs=[vmem, hbm, hbm, hbm],
        out_specs=(vmem, vmem, vmem),
        scratch_shapes=[
            pltpu.VMEM((NB, D), bf16),
            pltpu.VMEM((1, clip_dev), jnp.int32),
            pltpu.VMEM((3, D, D), bf16),
            pltpu.VMEM((F, ROWS // F, D), bf16),
            pltpu.VMEM((C, RC, ROWS), bf16),
            pltpu.VMEM((C, F, RC, ROWS), bf16),
            pltpu.VMEM((C, 3 * RC, F * ROWS), bf16),
            pltpu.VMEM((C, F, 2 * NB, (D + 128) // 2), bf16),
            pltpu.VMEM((caps, D), bf16),
            pltpu.VMEM((C, F, 2 * NB, (D + 128) // 2), bf16),
            pltpu.VMEM((caps, D), bf16),
            pltpu.VMEM((ROWS, D), f32),
            pltpu.VMEM((F, CC, ROWS), bf16),
            pltpu.VMEM((C, F, CC, ROWS), bf16),
            pltpu.VMEM((3 * RC, CC), f32),
            dma,
            dma,
            dma((3,)),
            dma((F,)),
            dma((F,)),
            dma((C,)),
            dma((C,)),
            dma((F,)),
            dma((F,)),
            dma((C,)),
            dma((C,)),
            dma((F,)),
            dma((F,)),
            dma((C,)),
            dma((C,)),
            dma((F,)),
            dma((F,)),
            dma((F,)),
            dma((F,)),
            dma((2, half, F)),
            dma((2, half, F)),
        ],
        compiler_params=pltpu.CompilerParams(
            collective_id=0, has_side_effects=True, vmem_limit_bytes=52 * 1024 * 1024
        ),
        cost_estimate=pl.CostEstimate(
            flops=4 * 3 * ROWS * D * D, bytes_accessed=8 * D * D, transcendentals=ROWS * D
        ),
    )(blocks, conv_weight, captions, positive.reshape(1, clip_dev))
    return loss[0, 0], grad_weight, grad_captions


def fits(C, F, frames, captions):
    clip_dev, fr_dev, D = frames.shape
    clips = clip_dev // F
    return (
        C == 8
        and F == 4
        and clips == 8
        and clip_dev % F == 0
        and captions.shape[0] == clips
        and fr_dev * F == FRAMES
        and D % (16 * C) == 0
        and D % 128 == 0
    )


def on_device(frames, conv_weight, captions, positive):
    C, F = lax.axis_size("clip"), lax.axis_size("frame")
    if fits(C, F, frames, captions):
        return fused(C, F, frames, conv_weight, captions, positive)
    return plain(frames, conv_weight, captions, positive)


def solution(mesh):
    placed = (P("clip", "frame", None), P(), P(("clip", "frame"), None), P("clip"))
    return jax.shard_map(
        on_device,
        mesh=mesh,
        in_specs=placed,
        out_specs=(P(), P(None, "clip", "frame"), P(("clip", "frame"), None)),
        check_vma=False,
    )
```

```python
import functools
import math

import jax
import jax.numpy as jnp
from jax import lax
from jax.experimental import pallas as pl
from jax.experimental.pallas import tpu as pltpu
from jax.sharding import PartitionSpec as P

FRAMES = 16


def with_halo(block, sides, width):
    for axis, dim in sides:
        count = lax.axis_size(axis)
        forward = [(i, i + 1) for i in range(count - 1)]
        backward = [(target, source) for source, target in forward]
        low = lax.ppermute(
            lax.slice_in_dim(block, block.shape[dim] - width, None, axis=dim), axis, forward
        )
        high = lax.ppermute(lax.slice_in_dim(block, 0, width, axis=dim), axis, backward)
        block = jnp.concatenate([low, block, high], axis=dim)
    return block


def plain(frames, conv_weight, captions, positive):
    clip_dev, fr_dev, width = frames.shape
    rows = clip_dev * fr_dev
    padded = with_halo(frames, (("frame", 1),), 1)
    shifted = [padded[:, k : k + fr_dev].reshape(rows, width) for k in range(3)]
    conv = jnp.dot(shifted[0], conv_weight[0], preferred_element_type=jnp.float32)
    conv = conv + jnp.dot(shifted[1], conv_weight[1], preferred_element_type=jnp.float32)
    conv = conv + jnp.dot(shifted[2], conv_weight[2], preferred_element_type=jnp.float32)
    hidden = frames.reshape(rows, width).astype(jnp.float32) + jax.nn.gelu(conv)
    partial_pool = jnp.sum(hidden.reshape(clip_dev, fr_dev, width), axis=1)
    pooled = lax.psum(partial_pool, "frame") / FRAMES
    pnorm = jnp.sqrt(jnp.sum(pooled * pooled, axis=1, keepdims=True) + 1e-06)
    unit = pooled / pnorm
    u_low = unit.astype(jnp.bfloat16)
    capf = captions.astype(jnp.float32)
    cnorm = jnp.sqrt(jnp.sum(capf * capf, axis=1, keepdims=True) + 1e-06)
    vunit = capf / cnorm
    v_low = vunit.astype(jnp.bfloat16)
    cap_dev = captions.shape[0]
    frame_pos = lax.axis_index("frame")
    piece = lax.all_gather(v_low, "clip", axis=0, tiled=True)
    count = piece.shape[0]
    place = jnp.arange(count, dtype=jnp.int32)
    ids = place // cap_dev * clip_dev + frame_pos * cap_dev + place % cap_dev
    logits = (
        10.0
        * lax.dot_general(
            u_low, piece, (((1,), (1,)), ((), ())), preferred_element_type=jnp.float32
        )
        - 10.0
    )
    match = (positive[:, None] == ids[None, :]).astype(jnp.float32)
    sign = 2.0 * match - 1.0
    total = jnp.sum(jax.nn.softplus(-sign * logits))
    coef = (10.0 * (jax.nn.sigmoid(logits) - match)).astype(jnp.bfloat16)
    du_acc = jnp.dot(coef, piece, preferred_element_type=jnp.float32)
    dv_piece = lax.dot_general(
        coef, u_low, (((0,), (0,)), ((), ())), preferred_element_type=jnp.float32
    )
    total, du_part, dv_all = (total, du_acc, dv_piece)
    dv_mine = lax.psum_scatter(dv_all, "clip", scatter_dimension=0, tiled=True)
    grad_captions = (dv_mine - vunit * jnp.sum(vunit * dv_mine, axis=1, keepdims=True)) / cnorm
    loss = lax.psum(total, ("clip", "frame")) / (clip_dev * lax.axis_size("clip"))
    du_full = lax.psum(du_part, "frame")
    dpooled = (du_full - unit * jnp.sum(unit * du_full, axis=1, keepdims=True)) / pnorm
    dhidden = jnp.broadcast_to((dpooled / FRAMES)[:, None, :], (clip_dev, fr_dev, width)).reshape(
        rows, width
    )
    _, pull = jax.vjp(jax.nn.gelu, conv)
    dconv = pull(dhidden)[0].astype(jnp.bfloat16).reshape(clip_dev, fr_dev, width)
    dconv_cols = lax.all_to_all(dconv, "frame", split_axis=2, concat_axis=1, tiled=True)
    block = fr_dev + 2
    col_width = dconv_cols.shape[2]
    every_block = lax.all_gather(padded, "frame", axis=1, tiled=True)
    groups = every_block.shape[1] // block
    blocks = every_block.reshape(clip_dev, groups, block, width)
    grads = dconv_cols.reshape(clip_dev, groups, fr_dev, col_width)
    parts = [
        jnp.einsum(
            "cgtd,cgte->de", blocks[:, :, k : k + fr_dev], grads, preferred_element_type=jnp.float32
        )
        for k in range(3)
    ]
    terms = jnp.stack(parts)
    grad_weight = lax.psum_scatter(terms, "clip", scatter_dimension=1, tiled=True)
    return (loss, grad_weight, grad_captions)


MESH = pl.DeviceIdType.MESH


def remote(src, dst, send_sem, recv_sem, device):
    return pltpu.make_async_remote_copy(
        src_ref=src,
        dst_ref=dst,
        send_sem=send_sem,
        recv_sem=recv_sem,
        device_id=device,
        device_id_type=MESH,
    )


def nt_dot(a, b):
    return lax.dot_general(a, b, (((1,), (1,)), ((), ())), preferred_element_type=jnp.float32)


def ring_to_clip(r, count):
    high = r // (count // 2)
    return 2 * r + high * (2 * count - 1 - 4 * r)


def pack(rows, extra):
    cut = (rows.shape[1] + extra.shape[1]) // 2
    bottom = jnp.concatenate([rows[:, cut:], extra], axis=1)
    return jnp.concatenate([rows[:, :cut], bottom], axis=0).astype(jnp.bfloat16)


def unpack(units, width):
    C, F, tall, cut = units.shape
    flat = units.reshape(C * F, tall, cut).astype(jnp.float32)
    top = flat[:, : tall // 2].reshape(C * F * tall // 2, cut)
    bottom = flat[:, tall // 2 :].reshape(C * F * tall // 2, cut)
    rows = jnp.concatenate([top, bottom[:, : width - cut]], axis=1)
    return rows.astype(jnp.bfloat16), bottom[:, width - cut :]


def fused_kernel(
    C,
    F,
    frames_ref,
    w_hbm,
    cap_hbm,
    pos_hbm,
    loss_ref,
    gw_ref,
    gc_ref,
    cap_ref,
    pos_ref,
    w_ref,
    x_rows,
    xt,
    xu,
    x3,
    vu,
    vb,
    uu,
    ub,
    slope,
    dt,
    dbuf,
    acc,
    cap_sem,
    pos_sem,
    own_sem,
    w_sem,
    fr_send,
    fr_recv,
    v1_send,
    v1_recv,
    v2_send,
    v2_recv,
    x1_send,
    x1_recv,
    x2_send,
    x2_recv,
    u1_send,
    u1_recv,
    u2_send,
    u2_recv,
    da_send,
    da_recv,
    ring_send,
    ring_recv,
):
    D = cap_ref.shape[1]
    NB = cap_ref.shape[0]
    T = FRAMES
    ROWS = T * NB
    part = ROWS // F
    RC = D // C
    CC = D // F
    c = lax.axis_index("clip")
    f = lax.axis_index("frame")
    half = C // 2
    z = c // 2
    pos = z + (c - 2 * z) * (C - 1 - 2 * z)
    right = ring_to_clip(lax.rem(pos + 1, C), C)
    left = ring_to_clip(lax.rem(pos + C - 1, C), C)

    cap_copy = pltpu.make_async_copy(cap_hbm, cap_ref, cap_sem)
    cap_copy.start()
    own_copy = pltpu.make_async_copy(frames_ref.at[f], x_rows.at[f], own_sem)
    own_copy.start()
    pos_copy = pltpu.make_async_copy(pos_hbm, pos_ref, pos_sem)
    pos_copy.start()
    w_copies = [pltpu.make_async_copy(w_hbm.at[k], w_ref.at[k], w_sem.at[k]) for k in range(3)]
    for copy in w_copies:
        copy.start()

    def cpeer(d):
        return lax.rem(c + d, C)

    def fpeer(d):
        return lax.rem(f + d, F)

    barrier = pltpu.get_barrier_semaphore()
    for d in range(1, C):
        pl.semaphore_signal(barrier, inc=1, device_id=(cpeer(d), f), device_id_type=MESH)
    for d in range(1, F):
        pl.semaphore_signal(barrier, inc=1, device_id=(c, fpeer(d)), device_id_type=MESH)

    cap_copy.wait()
    capf = cap_ref[...].astype(jnp.float32)
    cnorm = jnp.sqrt(jnp.sum(capf * capf, axis=1, keepdims=True) + 1e-06)
    vunit = capf / cnorm
    v_own = vunit.astype(jnp.bfloat16)
    vu[c, f] = pack(v_own.astype(jnp.float32), jnp.zeros((NB, 128), jnp.float32))
    pl.semaphore_wait(barrier, C + F - 2)

    sends = []

    def go(copy):
        copy.start()
        sends.append(copy)

    across = lax.rem(f + F // 2, F)
    beside = f + 1 - 2 * lax.rem(f, 2)
    diagonal = lax.rem(beside + F // 2, F)

    def spread(array, send_sem, recv_sem):
        slab = array.at[:, f]
        go(remote(slab, slab, send_sem.at[0], recv_sem.at[0], (c, across)))
        go(remote(slab, slab, send_sem.at[1], recv_sem.at[1], (c, beside)))

    def spread_on(array, send_sem, recv_sem):
        slab = array.at[:, across]
        remote(slab, slab, send_sem.at[0], recv_sem.at[0], (c, across)).wait_recv()
        go(remote(slab, slab, send_sem.at[2], recv_sem.at[2], (c, beside)))

    def spread_end(array, send_sem, recv_sem):
        for i, source in ((1, beside), (2, diagonal)):
            slab = array.at[:, source]
            remote(slab, slab, send_sem.at[i], recv_sem.at[i], (c, beside)).wait_recv()

    def clip_arrive(array, send_sem, recv_sem):
        for d in range(1, C):
            source = cpeer(C - d)
            slot = array.at[source, f]
            remote(slot, slot, send_sem.at[d], recv_sem.at[d], (source, f)).wait_recv()

    for d in range(1, F):
        go(
            remote(
                frames_ref.at[fpeer(d)],
                x_rows.at[f],
                fr_send.at[d],
                fr_recv.at[d],
                (c, fpeer(d)),
            )
        )
    for d in range(1, C):
        go(remote(vu.at[c, f], vu.at[c, f], v1_send.at[d], v1_recv.at[d], (cpeer(d), f)))

    for d in range(1, F):
        source = fpeer(F - d)
        remote(
            x_rows.at[source], x_rows.at[source], fr_send.at[d], fr_recv.at[d], (c, source)
        ).wait_recv()
    own_copy.wait()
    pos_copy.wait()
    xf = x_rows[...].reshape(ROWS, D).astype(jnp.float32)
    edge = jnp.zeros((NB, D), jnp.float32)
    before = jnp.concatenate([edge, xf[: ROWS - NB]], axis=0).astype(jnp.bfloat16)
    after = jnp.concatenate([xf[NB:], edge], axis=0).astype(jnp.bfloat16)
    w_copies[0].wait()
    conv = jnp.dot(before, w_ref[0], preferred_element_type=jnp.float32)
    xt[...] = xf.T.astype(jnp.bfloat16).reshape(C, RC, ROWS)
    for d in range(1, C):
        to = cpeer(d)
        go(remote(xt.at[to], xu.at[c, f], x1_send.at[d], x1_recv.at[d], (to, f)))
    xu[c, f] = xt[c]

    clip_arrive(vu, v1_send, v1_recv)
    spread(vu, v2_send, v2_recv)

    w_copies[1].wait()
    conv = conv + jnp.dot(
        x_rows[...].reshape(ROWS, D), w_ref[1], preferred_element_type=jnp.float32
    )
    w_copies[2].wait()
    conv = conv + jnp.dot(after, w_ref[2], preferred_element_type=jnp.float32)

    spread_on(vu, v2_send, v2_recv)

    scale = math.sqrt(2.0 / math.pi)
    square = conv * conv
    tanh = jnp.tanh(scale * conv * (1.0 + 0.044715 * square))
    cdf = 0.5 * (1.0 + tanh)
    slope[...] = cdf + (0.5 * scale) * conv * (1.0 - tanh * tanh) * (1.0 + 0.134145 * square)
    hidden = xf + conv * cdf
    pooled = jnp.sum(hidden.reshape(T, NB, D), axis=0) * (1.0 / T)
    pnorm = jnp.sqrt(jnp.sum(pooled * pooled, axis=1, keepdims=True) + 1e-06)
    unit = pooled / pnorm
    u_low = unit.astype(jnp.bfloat16)
    lanes = lax.broadcasted_iota(jnp.int32, (NB, F * NB), 1)
    mine = lanes == f * NB + lax.broadcasted_iota(jnp.int32, (NB, F * NB), 0)
    every_pos = jnp.broadcast_to(pos_ref[...].astype(jnp.float32), (NB, F * NB))
    pos_own = jnp.sum(jnp.where(mine, every_pos, 0.0), axis=1, keepdims=True)
    high = jnp.floor(pos_own * (1.0 / 128.0))
    lane = lax.broadcasted_iota(jnp.int32, (NB, 128), 1)
    split = jnp.where(lane < 64, high, pos_own - 128.0 * high)
    uu[c, f] = pack(u_low.astype(jnp.float32), split)
    for d in range(1, C):
        go(remote(uu.at[c, f], uu.at[c, f], u1_send.at[d], u1_recv.at[d], (cpeer(d), f)))

    clip_arrive(xu, x1_send, x1_recv)
    spread(xu, x2_send, x2_recv)

    spread_end(vu, v2_send, v2_recv)
    caps = C * F * NB
    vb[...] = unpack(vu[...], D)[0]
    logits = 10.0 * nt_dot(u_low, vb[...]) - 10.0
    ids = lax.broadcasted_iota(jnp.int32, (NB, caps), 1).astype(jnp.float32)
    match = jnp.where(pos_own == ids, 1.0, 0.0)
    coef = (10.0 * (1.0 / (1.0 + jnp.exp(-logits)) - match)).astype(jnp.bfloat16)
    du = jnp.dot(coef, vb[...], preferred_element_type=jnp.float32)
    dpooled = (du - unit * jnp.sum(unit * du, axis=1, keepdims=True)) / pnorm
    step = dpooled * (1.0 / T)
    dconv = (slope[...].reshape(T, NB, D) * step[None]).reshape(ROWS, D)
    dt[...] = dconv.T.astype(jnp.bfloat16).reshape(F, CC, ROWS)
    for d in range(1, F):
        to = fpeer(d)
        go(remote(dt.at[to], dbuf.at[c, f], da_send.at[d], da_recv.at[d], (c, to)))
    dbuf[c, f] = dt[f]

    ways = (right, left)

    def block_at(way, hop):
        return ring_to_clip(lax.rem(pos + (C - hop if way == 0 else hop), C), C)

    def units_at(way, hop):
        if hop < half:
            return range(F)
        return range(F // 2) if way == 0 else range(F // 2, F)

    def forward(way, hop, q):
        slot = dbuf.at[block_at(way, hop), fpeer(F - q)]
        go(
            remote(
                slot,
                slot,
                ring_send.at[way, hop, q],
                ring_recv.at[way, hop, q],
                (ways[way], f),
            )
        )

    def arrive(way, hop, q):
        slot = dbuf.at[block_at(way, hop), fpeer(F - q)]
        remote(
            slot,
            slot,
            ring_send.at[way, hop - 1, q],
            ring_recv.at[way, hop - 1, q],
            (ways[way], f),
        ).wait_recv()

    def relay(hop, *which):
        for q in which:
            for way in range(2):
                if q in units_at(way, hop):
                    arrive(way, hop, q)
                    if hop < half and q in units_at(way, hop + 1):
                        forward(way, hop, q)

    def block_term(block):
        rhs = jnp.concatenate([dbuf[block, i] for i in range(F)], axis=1)
        return nt_dot(x3[block], rhs)

    def add_block(block, first=False):
        if first:
            acc[...] = block_term(block)
        else:
            acc[...] += block_term(block)

    for q in range(F):
        if q:
            source = fpeer(F - q)
            slot = dbuf.at[c, source]
            remote(slot, slot, da_send.at[q], da_recv.at[q], (c, source)).wait_recv()
        for way in range(2):
            if q in units_at(way, 1):
                forward(way, 0, q)

    relay(1, 0)
    spread_on(xu, x2_send, x2_recv)
    spread_end(xu, x2_send, x2_recv)
    row = lax.broadcasted_iota(jnp.int32, (ROWS, ROWS), 0)
    col = lax.broadcasted_iota(jnp.int32, (ROWS, ROWS), 1)
    later = jnp.where(row == col - NB, 1.0, 0.0)
    earlier = jnp.where(row == col + NB, 1.0, 0.0)
    moves = jnp.concatenate([later, earlier], axis=1).astype(jnp.bfloat16)

    def shift(block, carry):
        units = xu[block]
        moved = jnp.dot(
            units.reshape(F * RC, ROWS), moves, preferred_element_type=jnp.float32
        ).astype(jnp.bfloat16)
        for i in range(F):
            lanes = slice(i * ROWS, (i + 1) * ROWS)
            rows = slice(i * RC, (i + 1) * RC)
            x3[block, 0:RC, lanes] = moved[rows, :ROWS]
            x3[block, RC : 2 * RC, lanes] = units[i]
            x3[block, 2 * RC :, lanes] = moved[rows, ROWS:]
        return carry

    quarter = C // 4
    lax.fori_loop(0, quarter, shift, 0)
    relay(1, 1)
    lax.fori_loop(quarter, 2 * quarter, shift, 0)
    relay(1, 2)
    lax.fori_loop(2 * quarter, 3 * quarter, shift, 0)
    relay(1, 3)
    clip_arrive(uu, u1_send, u1_recv)
    spread(uu, u2_send, u2_recv)
    lax.fori_loop(3 * quarter, C, shift, 0)
    relay(2, 0)
    add_block(c, first=True)
    relay(2, 1)
    add_block(block_at(0, 1))
    relay(2, 2)
    add_block(block_at(1, 1))
    relay(2, 3)
    spread_on(uu, u2_send, u2_recv)
    relay(3, 0)
    add_block(block_at(0, 2))
    relay(3, 1)
    add_block(block_at(1, 2))
    relay(3, 2)
    spread_end(uu, u2_send, u2_recv)
    u_all, halves = unpack(uu[...], D)
    ub[...] = u_all
    pos_all = 128.0 * halves[:, :1] + halves[:, 64:65]
    turned = halves.T
    pos_row = 128.0 * turned[:1] + turned[64:65]
    first_id = (c * F + f) * NB
    own_ids = (first_id + lax.broadcasted_iota(jnp.int32, (NB, caps), 0)).astype(jnp.float32)
    match_own = jnp.where(pos_row == own_ids, 1.0, 0.0)
    logits_own = 10.0 * nt_dot(v_own, ub[...]) - 10.0
    coef_own = (10.0 * (1.0 / (1.0 + jnp.exp(-logits_own)) - match_own)).astype(jnp.bfloat16)
    dv = jnp.dot(coef_own, ub[...], preferred_element_type=jnp.float32)
    gc_ref[...] = (dv - vunit * jnp.sum(vunit * dv, axis=1, keepdims=True)) / cnorm

    relay(3, 3)
    every = 10.0 * nt_dot(ub[...], vb[...]) - 10.0
    all_ids = lax.broadcasted_iota(jnp.int32, (caps, caps), 1).astype(jnp.float32)
    signed = jnp.where(pos_all == all_ids, -every, every)
    soft = jnp.maximum(signed, 0.0) + jnp.log1p(jnp.exp(-jnp.abs(signed)))
    total = jnp.sum(jnp.sum(soft, axis=0, keepdims=True), axis=1, keepdims=True)
    loss_ref[...] = jnp.broadcast_to(total * (1.0 / caps), loss_ref.shape)

    add_block(block_at(0, 3))
    add_block(block_at(1, 3))
    relay(4, *range(F))
    gw_ref[...] = (acc[...] + block_term(block_at(0, 4))).reshape(3, RC, CC)
    for copy in sends:
        copy.wait_send()


def fused(C, F, frames, conv_weight, captions, positive):
    clip_dev, fr_dev, D = frames.shape
    NB = clip_dev // F
    ROWS = FRAMES * NB
    RC, CC = D // C, D // F
    half = C // 2
    blocks = frames.reshape(F, NB, fr_dev, D).transpose(0, 2, 1, 3).reshape(F, fr_dev * NB, D)
    vmem = pl.BlockSpec(memory_space=pltpu.VMEM)
    hbm = pl.BlockSpec(memory_space=pltpu.HBM)
    dma = pltpu.SemaphoreType.DMA
    bf16, f32 = jnp.bfloat16, jnp.float32
    caps = C * F * NB
    loss, grad_weight, grad_captions = pl.pallas_call(
        functools.partial(fused_kernel, C, F),
        out_shape=(
            jax.ShapeDtypeStruct((8, 128), f32),
            jax.ShapeDtypeStruct((3, RC, CC), f32),
            jax.ShapeDtypeStruct((NB, D), f32),
        ),
        in_specs=[hbm, hbm, hbm, hbm],
        out_specs=(vmem, vmem, vmem),
        scratch_shapes=[
            pltpu.VMEM((NB, D), bf16),
            pltpu.VMEM((1, clip_dev), jnp.int32),
            pltpu.VMEM((3, D, D), bf16),
            pltpu.VMEM((F, ROWS // F, D), bf16),
            pltpu.VMEM((C, RC, ROWS), bf16),
            pltpu.VMEM((C, F, RC, ROWS), bf16),
            pltpu.VMEM((C, 3 * RC, F * ROWS), bf16),
            pltpu.VMEM((C, F, 2 * NB, (D + 128) // 2), bf16),
            pltpu.VMEM((caps, D), bf16),
            pltpu.VMEM((C, F, 2 * NB, (D + 128) // 2), bf16),
            pltpu.VMEM((caps, D), bf16),
            pltpu.VMEM((ROWS, D), f32),
            pltpu.VMEM((F, CC, ROWS), bf16),
            pltpu.VMEM((C, F, CC, ROWS), bf16),
            pltpu.VMEM((3 * RC, CC), f32),
            dma,
            dma,
            dma,
            dma((3,)),
            dma((F,)),
            dma((F,)),
            dma((C,)),
            dma((C,)),
            dma((F,)),
            dma((F,)),
            dma((C,)),
            dma((C,)),
            dma((F,)),
            dma((F,)),
            dma((C,)),
            dma((C,)),
            dma((F,)),
            dma((F,)),
            dma((F,)),
            dma((F,)),
            dma((2, half, F)),
            dma((2, half, F)),
        ],
        compiler_params=pltpu.CompilerParams(
            collective_id=0, has_side_effects=True, vmem_limit_bytes=60 * 1024 * 1024
        ),
        cost_estimate=pl.CostEstimate(
            flops=4 * 3 * ROWS * D * D, bytes_accessed=8 * D * D, transcendentals=ROWS * D
        ),
    )(blocks, conv_weight, captions, positive.reshape(1, clip_dev))
    return loss[0, 0], grad_weight, grad_captions


def fits(C, F, frames, captions):
    clip_dev, fr_dev, D = frames.shape
    clips = clip_dev // F
    return (
        C == 8
        and F == 4
        and clips == 8
        and clip_dev % F == 0
        and captions.shape[0] == clips
        and fr_dev * F == FRAMES
        and D % (16 * C) == 0
        and D % 128 == 0
    )


def on_device(frames, conv_weight, captions, positive):
    C, F = lax.axis_size("clip"), lax.axis_size("frame")
    if fits(C, F, frames, captions):
        return fused(C, F, frames, conv_weight, captions, positive)
    return plain(frames, conv_weight, captions, positive)


def solution(mesh):
    placed = (P("clip", "frame", None), P(), P(("clip", "frame"), None), P("clip"))
    return jax.shard_map(
        on_device,
        mesh=mesh,
        in_specs=placed,
        out_specs=(P(), P(None, "clip", "frame"), P(("clip", "frame"), None)),
        check_vma=False,
    )
```

```python
import functools
import math

import jax
import jax.numpy as jnp
from jax import lax
from jax.experimental import pallas as pl
from jax.experimental.pallas import tpu as pltpu
from jax.sharding import PartitionSpec as P

FRAMES = 16


def with_halo(block, sides, width):
    for axis, dim in sides:
        count = lax.axis_size(axis)
        forward = [(i, i + 1) for i in range(count - 1)]
        backward = [(target, source) for source, target in forward]
        low = lax.ppermute(
            lax.slice_in_dim(block, block.shape[dim] - width, None, axis=dim), axis, forward
        )
        high = lax.ppermute(lax.slice_in_dim(block, 0, width, axis=dim), axis, backward)
        block = jnp.concatenate([low, block, high], axis=dim)
    return block


def plain(frames, conv_weight, captions, positive):
    clip_dev, fr_dev, width = frames.shape
    rows = clip_dev * fr_dev
    padded = with_halo(frames, (("frame", 1),), 1)
    shifted = [padded[:, k : k + fr_dev].reshape(rows, width) for k in range(3)]
    conv = jnp.dot(shifted[0], conv_weight[0], preferred_element_type=jnp.float32)
    conv = conv + jnp.dot(shifted[1], conv_weight[1], preferred_element_type=jnp.float32)
    conv = conv + jnp.dot(shifted[2], conv_weight[2], preferred_element_type=jnp.float32)
    hidden = frames.reshape(rows, width).astype(jnp.float32) + jax.nn.gelu(conv)
    partial_pool = jnp.sum(hidden.reshape(clip_dev, fr_dev, width), axis=1)
    pooled = lax.psum(partial_pool, "frame") / FRAMES
    pnorm = jnp.sqrt(jnp.sum(pooled * pooled, axis=1, keepdims=True) + 1e-06)
    unit = pooled / pnorm
    u_low = unit.astype(jnp.bfloat16)
    capf = captions.astype(jnp.float32)
    cnorm = jnp.sqrt(jnp.sum(capf * capf, axis=1, keepdims=True) + 1e-06)
    vunit = capf / cnorm
    v_low = vunit.astype(jnp.bfloat16)
    cap_dev = captions.shape[0]
    frame_pos = lax.axis_index("frame")
    piece = lax.all_gather(v_low, "clip", axis=0, tiled=True)
    count = piece.shape[0]
    place = jnp.arange(count, dtype=jnp.int32)
    ids = place // cap_dev * clip_dev + frame_pos * cap_dev + place % cap_dev
    logits = (
        10.0
        * lax.dot_general(
            u_low, piece, (((1,), (1,)), ((), ())), preferred_element_type=jnp.float32
        )
        - 10.0
    )
    match = (positive[:, None] == ids[None, :]).astype(jnp.float32)
    sign = 2.0 * match - 1.0
    total = jnp.sum(jax.nn.softplus(-sign * logits))
    coef = (10.0 * (jax.nn.sigmoid(logits) - match)).astype(jnp.bfloat16)
    du_acc = jnp.dot(coef, piece, preferred_element_type=jnp.float32)
    dv_piece = lax.dot_general(
        coef, u_low, (((0,), (0,)), ((), ())), preferred_element_type=jnp.float32
    )
    total, du_part, dv_all = (total, du_acc, dv_piece)
    dv_mine = lax.psum_scatter(dv_all, "clip", scatter_dimension=0, tiled=True)
    grad_captions = (dv_mine - vunit * jnp.sum(vunit * dv_mine, axis=1, keepdims=True)) / cnorm
    loss = lax.psum(total, ("clip", "frame")) / (clip_dev * lax.axis_size("clip"))
    du_full = lax.psum(du_part, "frame")
    dpooled = (du_full - unit * jnp.sum(unit * du_full, axis=1, keepdims=True)) / pnorm
    dhidden = jnp.broadcast_to((dpooled / FRAMES)[:, None, :], (clip_dev, fr_dev, width)).reshape(
        rows, width
    )
    _, pull = jax.vjp(jax.nn.gelu, conv)
    dconv = pull(dhidden)[0].astype(jnp.bfloat16).reshape(clip_dev, fr_dev, width)
    dconv_cols = lax.all_to_all(dconv, "frame", split_axis=2, concat_axis=1, tiled=True)
    block = fr_dev + 2
    col_width = dconv_cols.shape[2]
    every_block = lax.all_gather(padded, "frame", axis=1, tiled=True)
    groups = every_block.shape[1] // block
    blocks = every_block.reshape(clip_dev, groups, block, width)
    grads = dconv_cols.reshape(clip_dev, groups, fr_dev, col_width)
    parts = [
        jnp.einsum(
            "cgtd,cgte->de", blocks[:, :, k : k + fr_dev], grads, preferred_element_type=jnp.float32
        )
        for k in range(3)
    ]
    terms = jnp.stack(parts)
    grad_weight = lax.psum_scatter(terms, "clip", scatter_dimension=1, tiled=True)
    return (loss, grad_weight, grad_captions)


MESH = pl.DeviceIdType.MESH


def remote(src, dst, send_sem, recv_sem, device):
    return pltpu.make_async_remote_copy(
        src_ref=src,
        dst_ref=dst,
        send_sem=send_sem,
        recv_sem=recv_sem,
        device_id=device,
        device_id_type=MESH,
    )


def nt_dot(a, b):
    return lax.dot_general(a, b, (((1,), (1,)), ((), ())), preferred_element_type=jnp.float32)


def ring_to_clip(r, count):
    high = r // (count // 2)
    return 2 * r + high * (2 * count - 1 - 4 * r)


def pack(rows, extra):
    cut = (rows.shape[1] + extra.shape[1]) // 2
    bottom = jnp.concatenate([rows[:, cut:], extra], axis=1)
    return jnp.concatenate([rows[:, :cut], bottom], axis=0).astype(jnp.bfloat16)


def unpack(units, width):
    C, F, tall, cut = units.shape
    flat = units.reshape(C * F, tall, cut).astype(jnp.float32)
    top = flat[:, : tall // 2].reshape(C * F * tall // 2, cut)
    bottom = flat[:, tall // 2 :].reshape(C * F * tall // 2, cut)
    rows = jnp.concatenate([top, bottom[:, : width - cut]], axis=1)
    return rows.astype(jnp.bfloat16), bottom[:, width - cut :]


def fused_kernel(
    C,
    F,
    frames_ref,
    w_hbm,
    cap_hbm,
    pos_hbm,
    loss_ref,
    gw_ref,
    gc_ref,
    cap_ref,
    pos_ref,
    w_ref,
    x_rows,
    xt,
    xu,
    x3,
    vu,
    vb,
    uu,
    ub,
    slope,
    dt,
    dbuf,
    acc,
    cap_sem,
    pos_sem,
    own_sem,
    w_sem,
    fr_send,
    fr_recv,
    v1_send,
    v1_recv,
    v2_send,
    v2_recv,
    x1_send,
    x1_recv,
    x2_send,
    x2_recv,
    u1_send,
    u1_recv,
    u2_send,
    u2_recv,
    da_send,
    da_recv,
    ring_send,
    ring_recv,
):
    D = cap_ref.shape[1]
    NB = cap_ref.shape[0]
    T = FRAMES
    ROWS = T * NB
    part = ROWS // F
    RC = D // C
    CC = D // F
    c = lax.axis_index("clip")
    f = lax.axis_index("frame")
    half = C // 2
    z = c // 2
    pos = z + (c - 2 * z) * (C - 1 - 2 * z)
    right = ring_to_clip(lax.rem(pos + 1, C), C)
    left = ring_to_clip(lax.rem(pos + C - 1, C), C)

    cap_copy = pltpu.make_async_copy(cap_hbm, cap_ref, cap_sem)
    cap_copy.start()
    own_copy = pltpu.make_async_copy(frames_ref.at[f], x_rows.at[f], own_sem)
    own_copy.start()
    pos_copy = pltpu.make_async_copy(pos_hbm, pos_ref, pos_sem)
    pos_copy.start()
    w_copies = [pltpu.make_async_copy(w_hbm.at[k], w_ref.at[k], w_sem.at[k]) for k in range(3)]
    for copy in w_copies:
        copy.start()

    def cpeer(d):
        return lax.rem(c + d, C)

    def fpeer(d):
        return lax.rem(f + d, F)

    barrier = pltpu.get_barrier_semaphore()
    for d in range(1, C):
        pl.semaphore_signal(barrier, inc=1, device_id=(cpeer(d), f), device_id_type=MESH)
    for d in range(1, F):
        pl.semaphore_signal(barrier, inc=1, device_id=(c, fpeer(d)), device_id_type=MESH)

    cap_copy.wait()
    capf = cap_ref[...].astype(jnp.float32)
    cnorm = jnp.sqrt(jnp.sum(capf * capf, axis=1, keepdims=True) + 1e-06)
    vunit = capf / cnorm
    v_own = vunit.astype(jnp.bfloat16)
    vu[c, f] = pack(v_own.astype(jnp.float32), jnp.zeros((NB, 128), jnp.float32))
    pl.semaphore_wait(barrier, C + F - 2)

    sends = []

    def go(copy):
        copy.start()
        sends.append(copy)

    across = lax.rem(f + F // 2, F)
    beside = f + 1 - 2 * lax.rem(f, 2)
    diagonal = lax.rem(beside + F // 2, F)

    def spread(array, send_sem, recv_sem):
        slab = array.at[:, f]
        go(remote(slab, slab, send_sem.at[0], recv_sem.at[0], (c, across)))
        go(remote(slab, slab, send_sem.at[1], recv_sem.at[1], (c, beside)))

    def spread_on(array, send_sem, recv_sem):
        slab = array.at[:, across]
        remote(slab, slab, send_sem.at[0], recv_sem.at[0], (c, across)).wait_recv()
        go(remote(slab, slab, send_sem.at[2], recv_sem.at[2], (c, beside)))

    def spread_end(array, send_sem, recv_sem):
        for i, source in ((1, beside), (2, diagonal)):
            slab = array.at[:, source]
            remote(slab, slab, send_sem.at[i], recv_sem.at[i], (c, beside)).wait_recv()

    def clip_arrive(array, send_sem, recv_sem):
        for d in range(1, C):
            source = cpeer(C - d)
            slot = array.at[source, f]
            remote(slot, slot, send_sem.at[d], recv_sem.at[d], (source, f)).wait_recv()

    for d in range(1, F):
        go(
            remote(
                frames_ref.at[fpeer(d)],
                x_rows.at[f],
                fr_send.at[d],
                fr_recv.at[d],
                (c, fpeer(d)),
            )
        )
    for d in range(1, C):
        go(remote(vu.at[c, f], vu.at[c, f], v1_send.at[d], v1_recv.at[d], (cpeer(d), f)))

    for d in range(1, F):
        source = fpeer(F - d)
        remote(
            x_rows.at[source], x_rows.at[source], fr_send.at[d], fr_recv.at[d], (c, source)
        ).wait_recv()
    own_copy.wait()
    pos_copy.wait()
    xf = x_rows[...].reshape(ROWS, D).astype(jnp.float32)
    edge = jnp.zeros((NB, D), jnp.float32)
    before = jnp.concatenate([edge, xf[: ROWS - NB]], axis=0).astype(jnp.bfloat16)
    after = jnp.concatenate([xf[NB:], edge], axis=0).astype(jnp.bfloat16)
    w_copies[0].wait()
    conv = jnp.dot(before, w_ref[0], preferred_element_type=jnp.float32)
    xt[...] = xf.T.astype(jnp.bfloat16).reshape(C, RC, ROWS)
    for d in range(1, C):
        to = cpeer(d)
        go(remote(xt.at[to], xu.at[c, f], x1_send.at[d], x1_recv.at[d], (to, f)))
    xu[c, f] = xt[c]

    clip_arrive(vu, v1_send, v1_recv)
    spread(vu, v2_send, v2_recv)

    w_copies[1].wait()
    conv = conv + jnp.dot(
        x_rows[...].reshape(ROWS, D), w_ref[1], preferred_element_type=jnp.float32
    )
    w_copies[2].wait()
    conv = conv + jnp.dot(after, w_ref[2], preferred_element_type=jnp.float32)

    spread_on(vu, v2_send, v2_recv)

    scale = math.sqrt(2.0 / math.pi)
    square = conv * conv
    tanh = jnp.tanh(scale * conv * (1.0 + 0.044715 * square))
    cdf = 0.5 * (1.0 + tanh)
    slope[...] = cdf + (0.5 * scale) * conv * (1.0 - tanh * tanh) * (1.0 + 0.134145 * square)
    hidden = xf + conv * cdf
    pooled = jnp.sum(hidden.reshape(T, NB, D), axis=0) * (1.0 / T)
    pnorm = jnp.sqrt(jnp.sum(pooled * pooled, axis=1, keepdims=True) + 1e-06)
    unit = pooled / pnorm
    u_low = unit.astype(jnp.bfloat16)
    lanes = lax.broadcasted_iota(jnp.int32, (NB, F * NB), 1)
    mine = lanes == f * NB + lax.broadcasted_iota(jnp.int32, (NB, F * NB), 0)
    every_pos = jnp.broadcast_to(pos_ref[...].astype(jnp.float32), (NB, F * NB))
    pos_own = jnp.sum(jnp.where(mine, every_pos, 0.0), axis=1, keepdims=True)
    high = jnp.floor(pos_own * (1.0 / 128.0))
    lane = lax.broadcasted_iota(jnp.int32, (NB, 128), 1)
    split = jnp.where(lane < 64, high, pos_own - 128.0 * high)
    uu[c, f] = pack(u_low.astype(jnp.float32), split)
    for d in range(1, C):
        go(remote(uu.at[c, f], uu.at[c, f], u1_send.at[d], u1_recv.at[d], (cpeer(d), f)))

    spread_end(vu, v2_send, v2_recv)
    caps = C * F * NB
    vb[...] = unpack(vu[...], D)[0]
    logits = 10.0 * nt_dot(u_low, vb[...]) - 10.0
    ids = lax.broadcasted_iota(jnp.int32, (NB, caps), 1).astype(jnp.float32)
    match = jnp.where(pos_own == ids, 1.0, 0.0)
    coef = (10.0 * (1.0 / (1.0 + jnp.exp(-logits)) - match)).astype(jnp.bfloat16)
    du = jnp.dot(coef, vb[...], preferred_element_type=jnp.float32)
    dpooled = (du - unit * jnp.sum(unit * du, axis=1, keepdims=True)) / pnorm
    step = dpooled * (1.0 / T)
    dconv = (slope[...].reshape(T, NB, D) * step[None]).reshape(ROWS, D)
    dt[...] = dconv.T.astype(jnp.bfloat16).reshape(F, CC, ROWS)
    for d in range(1, F):
        to = fpeer(d)
        go(remote(dt.at[to], dbuf.at[c, f], da_send.at[d], da_recv.at[d], (c, to)))
    dbuf[c, f] = dt[f]

    ways = (right, left)

    def block_at(way, hop):
        return ring_to_clip(lax.rem(pos + (C - hop if way == 0 else hop), C), C)

    def units_at(way, hop):
        if hop < half:
            return range(F)
        return range(F // 2) if way == 0 else range(F // 2, F)

    def forward(way, hop, q):
        slot = dbuf.at[block_at(way, hop), fpeer(F - q)]
        go(
            remote(
                slot,
                slot,
                ring_send.at[way, hop, q],
                ring_recv.at[way, hop, q],
                (ways[way], f),
            )
        )

    def arrive(way, hop, q):
        slot = dbuf.at[block_at(way, hop), fpeer(F - q)]
        remote(
            slot,
            slot,
            ring_send.at[way, hop - 1, q],
            ring_recv.at[way, hop - 1, q],
            (ways[way], f),
        ).wait_recv()

    def relay(hop, *which):
        for q in which:
            for way in range(2):
                if q in units_at(way, hop):
                    arrive(way, hop, q)
                    if hop < half and q in units_at(way, hop + 1):
                        forward(way, hop, q)

    def block_term(block):
        rhs = jnp.concatenate([dbuf[block, i] for i in range(F)], axis=1)
        return nt_dot(x3[block], rhs)

    def add_block(block, first=False):
        if first:
            acc[...] = block_term(block)
        else:
            acc[...] += block_term(block)

    for q in range(F):
        if q:
            source = fpeer(F - q)
            slot = dbuf.at[c, source]
            remote(slot, slot, da_send.at[q], da_recv.at[q], (c, source)).wait_recv()
        for way in range(2):
            if q in units_at(way, 1):
                forward(way, 0, q)

    clip_arrive(xu, x1_send, x1_recv)
    spread(xu, x2_send, x2_recv)
    relay(1, 0)
    clip_arrive(uu, u1_send, u1_recv)
    spread(uu, u2_send, u2_recv)
    relay(1, 1, 2)
    spread_on(xu, x2_send, x2_recv)
    relay(1, 3)
    spread_end(xu, x2_send, x2_recv)
    row = lax.broadcasted_iota(jnp.int32, (ROWS, ROWS), 0)
    col = lax.broadcasted_iota(jnp.int32, (ROWS, ROWS), 1)
    later = jnp.where(row == col - NB, 1.0, 0.0)
    earlier = jnp.where(row == col + NB, 1.0, 0.0)
    moves = jnp.concatenate([later, earlier], axis=1).astype(jnp.bfloat16)

    def shift(block, carry):
        units = xu[block]
        moved = jnp.dot(
            units.reshape(F * RC, ROWS), moves, preferred_element_type=jnp.float32
        ).astype(jnp.bfloat16)
        for i in range(F):
            lanes = slice(i * ROWS, (i + 1) * ROWS)
            rows = slice(i * RC, (i + 1) * RC)
            x3[block, 0:RC, lanes] = moved[rows, :ROWS]
            x3[block, RC : 2 * RC, lanes] = units[i]
            x3[block, 2 * RC :, lanes] = moved[rows, ROWS:]
        return carry

    quarter = C // 4
    for q in range(4):
        lax.fori_loop(q * quarter, (q + 1) * quarter, shift, 0)
        relay(2, q)
    add_block(c, first=True)
    spread_on(uu, u2_send, u2_recv)
    add_block(block_at(0, 1))
    relay(3, 0)
    add_block(block_at(1, 1))
    relay(3, 1)
    add_block(block_at(0, 2))
    relay(3, 2)
    add_block(block_at(1, 2))
    relay(3, 3)
    spread_end(uu, u2_send, u2_recv)
    u_all, halves = unpack(uu[...], D)
    ub[...] = u_all
    pos_all = 128.0 * halves[:, :1] + halves[:, 64:65]
    turned = halves.T
    pos_row = 128.0 * turned[:1] + turned[64:65]
    first_id = (c * F + f) * NB
    own_ids = (first_id + lax.broadcasted_iota(jnp.int32, (NB, caps), 0)).astype(jnp.float32)
    match_own = jnp.where(pos_row == own_ids, 1.0, 0.0)
    logits_own = 10.0 * nt_dot(v_own, ub[...]) - 10.0
    coef_own = (10.0 * (1.0 / (1.0 + jnp.exp(-logits_own)) - match_own)).astype(jnp.bfloat16)
    dv = jnp.dot(coef_own, ub[...], preferred_element_type=jnp.float32)
    gc_ref[...] = (dv - vunit * jnp.sum(vunit * dv, axis=1, keepdims=True)) / cnorm

    every = 10.0 * nt_dot(ub[...], vb[...]) - 10.0
    all_ids = lax.broadcasted_iota(jnp.int32, (caps, caps), 1).astype(jnp.float32)
    signed = jnp.where(pos_all == all_ids, -every, every)
    soft = jnp.maximum(signed, 0.0) + jnp.log1p(jnp.exp(-jnp.abs(signed)))
    total = jnp.sum(jnp.sum(soft, axis=0, keepdims=True), axis=1, keepdims=True)
    loss_ref[...] = jnp.broadcast_to(total * (1.0 / caps), loss_ref.shape)

    add_block(block_at(0, 3))
    add_block(block_at(1, 3))
    relay(4, *range(F))
    gw_ref[...] = (acc[...] + block_term(block_at(0, 4))).reshape(3, RC, CC)
    for copy in sends:
        copy.wait_send()


def fused(C, F, frames, conv_weight, captions, positive):
    clip_dev, fr_dev, D = frames.shape
    NB = clip_dev // F
    ROWS = FRAMES * NB
    RC, CC = D // C, D // F
    half = C // 2
    blocks = frames.reshape(F, NB, fr_dev, D).transpose(0, 2, 1, 3).reshape(F, fr_dev * NB, D)
    vmem = pl.BlockSpec(memory_space=pltpu.VMEM)
    hbm = pl.BlockSpec(memory_space=pltpu.HBM)
    dma = pltpu.SemaphoreType.DMA
    bf16, f32 = jnp.bfloat16, jnp.float32
    caps = C * F * NB
    loss, grad_weight, grad_captions = pl.pallas_call(
        functools.partial(fused_kernel, C, F),
        out_shape=(
            jax.ShapeDtypeStruct((8, 128), f32),
            jax.ShapeDtypeStruct((3, RC, CC), f32),
            jax.ShapeDtypeStruct((NB, D), f32),
        ),
        in_specs=[hbm, hbm, hbm, hbm],
        out_specs=(vmem, vmem, vmem),
        scratch_shapes=[
            pltpu.VMEM((NB, D), bf16),
            pltpu.VMEM((1, clip_dev), jnp.int32),
            pltpu.VMEM((3, D, D), bf16),
            pltpu.VMEM((F, ROWS // F, D), bf16),
            pltpu.VMEM((C, RC, ROWS), bf16),
            pltpu.VMEM((C, F, RC, ROWS), bf16),
            pltpu.VMEM((C, 3 * RC, F * ROWS), bf16),
            pltpu.VMEM((C, F, 2 * NB, (D + 128) // 2), bf16),
            pltpu.VMEM((caps, D), bf16),
            pltpu.VMEM((C, F, 2 * NB, (D + 128) // 2), bf16),
            pltpu.VMEM((caps, D), bf16),
            pltpu.VMEM((ROWS, D), f32),
            pltpu.VMEM((F, CC, ROWS), bf16),
            pltpu.VMEM((C, F, CC, ROWS), bf16),
            pltpu.VMEM((3 * RC, CC), f32),
            dma,
            dma,
            dma,
            dma((3,)),
            dma((F,)),
            dma((F,)),
            dma((C,)),
            dma((C,)),
            dma((F,)),
            dma((F,)),
            dma((C,)),
            dma((C,)),
            dma((F,)),
            dma((F,)),
            dma((C,)),
            dma((C,)),
            dma((F,)),
            dma((F,)),
            dma((F,)),
            dma((F,)),
            dma((2, half, F)),
            dma((2, half, F)),
        ],
        compiler_params=pltpu.CompilerParams(
            collective_id=0, has_side_effects=True, vmem_limit_bytes=52 * 1024 * 1024
        ),
        cost_estimate=pl.CostEstimate(
            flops=4 * 3 * ROWS * D * D, bytes_accessed=8 * D * D, transcendentals=ROWS * D
        ),
    )(blocks, conv_weight, captions, positive.reshape(1, clip_dev))
    return loss[0, 0], grad_weight, grad_captions


def fits(C, F, frames, captions):
    clip_dev, fr_dev, D = frames.shape
    clips = clip_dev // F
    return (
        C == 8
        and F == 4
        and clips == 8
        and clip_dev % F == 0
        and captions.shape[0] == clips
        and fr_dev * F == FRAMES
        and D % (16 * C) == 0
        and D % 128 == 0
    )


def on_device(frames, conv_weight, captions, positive):
    C, F = lax.axis_size("clip"), lax.axis_size("frame")
    if fits(C, F, frames, captions):
        return fused(C, F, frames, conv_weight, captions, positive)
    return plain(frames, conv_weight, captions, positive)


def solution(mesh):
    placed = (P("clip", "frame", None), P(), P(("clip", "frame"), None), P("clip"))
    return jax.shard_map(
        on_device,
        mesh=mesh,
        in_specs=placed,
        out_specs=(P(), P(None, "clip", "frame"), P(("clip", "frame"), None)),
        check_vma=False,
    )
```

```python
import functools
import math

import jax
import jax.numpy as jnp
from jax import lax
from jax.experimental import pallas as pl
from jax.experimental.pallas import tpu as pltpu
from jax.sharding import PartitionSpec as P

FRAMES = 16


def with_halo(block, sides, width):
    for axis, dim in sides:
        count = lax.axis_size(axis)
        forward = [(i, i + 1) for i in range(count - 1)]
        backward = [(target, source) for source, target in forward]
        low = lax.ppermute(
            lax.slice_in_dim(block, block.shape[dim] - width, None, axis=dim), axis, forward
        )
        high = lax.ppermute(lax.slice_in_dim(block, 0, width, axis=dim), axis, backward)
        block = jnp.concatenate([low, block, high], axis=dim)
    return block


def plain(frames, conv_weight, captions, positive):
    clip_dev, fr_dev, width = frames.shape
    rows = clip_dev * fr_dev
    padded = with_halo(frames, (("frame", 1),), 1)
    shifted = [padded[:, k : k + fr_dev].reshape(rows, width) for k in range(3)]
    conv = jnp.dot(shifted[0], conv_weight[0], preferred_element_type=jnp.float32)
    conv = conv + jnp.dot(shifted[1], conv_weight[1], preferred_element_type=jnp.float32)
    conv = conv + jnp.dot(shifted[2], conv_weight[2], preferred_element_type=jnp.float32)
    hidden = frames.reshape(rows, width).astype(jnp.float32) + jax.nn.gelu(conv)
    partial_pool = jnp.sum(hidden.reshape(clip_dev, fr_dev, width), axis=1)
    pooled = lax.psum(partial_pool, "frame") / FRAMES
    pnorm = jnp.sqrt(jnp.sum(pooled * pooled, axis=1, keepdims=True) + 1e-06)
    unit = pooled / pnorm
    u_low = unit.astype(jnp.bfloat16)
    capf = captions.astype(jnp.float32)
    cnorm = jnp.sqrt(jnp.sum(capf * capf, axis=1, keepdims=True) + 1e-06)
    vunit = capf / cnorm
    v_low = vunit.astype(jnp.bfloat16)
    cap_dev = captions.shape[0]
    frame_pos = lax.axis_index("frame")
    piece = lax.all_gather(v_low, "clip", axis=0, tiled=True)
    count = piece.shape[0]
    place = jnp.arange(count, dtype=jnp.int32)
    ids = place // cap_dev * clip_dev + frame_pos * cap_dev + place % cap_dev
    logits = (
        10.0
        * lax.dot_general(
            u_low, piece, (((1,), (1,)), ((), ())), preferred_element_type=jnp.float32
        )
        - 10.0
    )
    match = (positive[:, None] == ids[None, :]).astype(jnp.float32)
    sign = 2.0 * match - 1.0
    total = jnp.sum(jax.nn.softplus(-sign * logits))
    coef = (10.0 * (jax.nn.sigmoid(logits) - match)).astype(jnp.bfloat16)
    du_acc = jnp.dot(coef, piece, preferred_element_type=jnp.float32)
    dv_piece = lax.dot_general(
        coef, u_low, (((0,), (0,)), ((), ())), preferred_element_type=jnp.float32
    )
    total, du_part, dv_all = (total, du_acc, dv_piece)
    dv_mine = lax.psum_scatter(dv_all, "clip", scatter_dimension=0, tiled=True)
    grad_captions = (dv_mine - vunit * jnp.sum(vunit * dv_mine, axis=1, keepdims=True)) / cnorm
    loss = lax.psum(total, ("clip", "frame")) / (clip_dev * lax.axis_size("clip"))
    du_full = lax.psum(du_part, "frame")
    dpooled = (du_full - unit * jnp.sum(unit * du_full, axis=1, keepdims=True)) / pnorm
    dhidden = jnp.broadcast_to((dpooled / FRAMES)[:, None, :], (clip_dev, fr_dev, width)).reshape(
        rows, width
    )
    _, pull = jax.vjp(jax.nn.gelu, conv)
    dconv = pull(dhidden)[0].astype(jnp.bfloat16).reshape(clip_dev, fr_dev, width)
    dconv_cols = lax.all_to_all(dconv, "frame", split_axis=2, concat_axis=1, tiled=True)
    block = fr_dev + 2
    col_width = dconv_cols.shape[2]
    every_block = lax.all_gather(padded, "frame", axis=1, tiled=True)
    groups = every_block.shape[1] // block
    blocks = every_block.reshape(clip_dev, groups, block, width)
    grads = dconv_cols.reshape(clip_dev, groups, fr_dev, col_width)
    parts = [
        jnp.einsum(
            "cgtd,cgte->de", blocks[:, :, k : k + fr_dev], grads, preferred_element_type=jnp.float32
        )
        for k in range(3)
    ]
    terms = jnp.stack(parts)
    grad_weight = lax.psum_scatter(terms, "clip", scatter_dimension=1, tiled=True)
    return (loss, grad_weight, grad_captions)


MESH = pl.DeviceIdType.MESH


def remote(src, dst, send_sem, recv_sem, device):
    return pltpu.make_async_remote_copy(
        src_ref=src,
        dst_ref=dst,
        send_sem=send_sem,
        recv_sem=recv_sem,
        device_id=device,
        device_id_type=MESH,
    )


def nt_dot(a, b):
    return lax.dot_general(a, b, (((1,), (1,)), ((), ())), preferred_element_type=jnp.float32)


def ring_to_clip(r, count):
    high = r // (count // 2)
    return 2 * r + high * (2 * count - 1 - 4 * r)


def pack(rows, extra):
    cut = (rows.shape[1] + extra.shape[1]) // 2
    bottom = jnp.concatenate([rows[:, cut:], extra], axis=1)
    return jnp.concatenate([rows[:, :cut], bottom], axis=0).astype(jnp.bfloat16)


def unpack(units, width):
    C, F, tall, cut = units.shape
    flat = units.reshape(C * F, tall, cut).astype(jnp.float32)
    top = flat[:, : tall // 2].reshape(C * F * tall // 2, cut)
    bottom = flat[:, tall // 2 :].reshape(C * F * tall // 2, cut)
    rows = jnp.concatenate([top, bottom[:, : width - cut]], axis=1)
    return rows.astype(jnp.bfloat16), bottom[:, width - cut :]


def fused_kernel(
    C,
    F,
    frames_ref,
    w_hbm,
    cap_hbm,
    pos_hbm,
    loss_ref,
    gw_ref,
    gc_ref,
    cap_ref,
    pos_ref,
    w_ref,
    x_rows,
    xt,
    xu,
    x3,
    vu,
    vb,
    uu,
    ub,
    slope,
    dt,
    dbuf,
    acc,
    cap_sem,
    pos_sem,
    own_sem,
    w_sem,
    fr_send,
    fr_recv,
    v1_send,
    v1_recv,
    v2_send,
    v2_recv,
    x1_send,
    x1_recv,
    x2_send,
    x2_recv,
    u1_send,
    u1_recv,
    u2_send,
    u2_recv,
    da_send,
    da_recv,
    ring_send,
    ring_recv,
):
    D = cap_ref.shape[1]
    NB = cap_ref.shape[0]
    T = FRAMES
    ROWS = T * NB
    part = ROWS // F
    RC = D // C
    CC = D // F
    c = lax.axis_index("clip")
    f = lax.axis_index("frame")
    half = C // 2
    z = c // 2
    pos = z + (c - 2 * z) * (C - 1 - 2 * z)
    right = ring_to_clip(lax.rem(pos + 1, C), C)
    left = ring_to_clip(lax.rem(pos + C - 1, C), C)

    cap_copy = pltpu.make_async_copy(cap_hbm, cap_ref, cap_sem)
    cap_copy.start()
    own_copy = pltpu.make_async_copy(frames_ref.at[f], x_rows.at[f], own_sem)
    own_copy.start()
    pos_copy = pltpu.make_async_copy(pos_hbm, pos_ref, pos_sem)
    pos_copy.start()
    w_copies = [pltpu.make_async_copy(w_hbm.at[k], w_ref.at[k], w_sem.at[k]) for k in range(3)]
    for copy in w_copies:
        copy.start()

    def cpeer(d):
        return lax.rem(c + d, C)

    def fpeer(d):
        return lax.rem(f + d, F)

    barrier = pltpu.get_barrier_semaphore()
    for d in range(1, C):
        pl.semaphore_signal(barrier, inc=1, device_id=(cpeer(d), f), device_id_type=MESH)
    for d in range(1, F):
        pl.semaphore_signal(barrier, inc=1, device_id=(c, fpeer(d)), device_id_type=MESH)

    cap_copy.wait()
    capf = cap_ref[...].astype(jnp.float32)
    cnorm = jnp.sqrt(jnp.sum(capf * capf, axis=1, keepdims=True) + 1e-06)
    vunit = capf / cnorm
    v_own = vunit.astype(jnp.bfloat16)
    vu[c, f] = pack(v_own.astype(jnp.float32), jnp.zeros((NB, 128), jnp.float32))
    pl.semaphore_wait(barrier, C + F - 2)

    sends = []

    def go(copy):
        copy.start()
        sends.append(copy)

    across = lax.rem(f + F // 2, F)
    beside = f + 1 - 2 * lax.rem(f, 2)
    diagonal = lax.rem(beside + F // 2, F)

    def spread(array, send_sem, recv_sem):
        slab = array.at[:, f]
        go(remote(slab, slab, send_sem.at[0], recv_sem.at[0], (c, across)))
        go(remote(slab, slab, send_sem.at[1], recv_sem.at[1], (c, beside)))

    def spread_on(array, send_sem, recv_sem):
        slab = array.at[:, across]
        remote(slab, slab, send_sem.at[0], recv_sem.at[0], (c, across)).wait_recv()
        go(remote(slab, slab, send_sem.at[2], recv_sem.at[2], (c, beside)))

    def spread_end(array, send_sem, recv_sem):
        for i, source in ((1, beside), (2, diagonal)):
            slab = array.at[:, source]
            remote(slab, slab, send_sem.at[i], recv_sem.at[i], (c, beside)).wait_recv()

    def clip_arrive(array, send_sem, recv_sem):
        for d in range(1, C):
            source = cpeer(C - d)
            slot = array.at[source, f]
            remote(slot, slot, send_sem.at[d], recv_sem.at[d], (source, f)).wait_recv()

    for d in range(1, F):
        go(
            remote(
                frames_ref.at[fpeer(d)],
                x_rows.at[f],
                fr_send.at[d],
                fr_recv.at[d],
                (c, fpeer(d)),
            )
        )
    for d in range(1, C):
        go(remote(vu.at[c, f], vu.at[c, f], v1_send.at[d], v1_recv.at[d], (cpeer(d), f)))

    for d in range(1, F):
        source = fpeer(F - d)
        remote(
            x_rows.at[source], x_rows.at[source], fr_send.at[d], fr_recv.at[d], (c, source)
        ).wait_recv()
    own_copy.wait()
    pos_copy.wait()
    xf = x_rows[...].reshape(ROWS, D).astype(jnp.float32)
    edge = jnp.zeros((NB, D), jnp.float32)
    before = jnp.concatenate([edge, xf[: ROWS - NB]], axis=0).astype(jnp.bfloat16)
    after = jnp.concatenate([xf[NB:], edge], axis=0).astype(jnp.bfloat16)
    w_copies[0].wait()
    clip_arrive(vu, v1_send, v1_recv)
    spread(vu, v2_send, v2_recv)
    conv = jnp.dot(before, w_ref[0], preferred_element_type=jnp.float32)
    xt[...] = xf.T.astype(jnp.bfloat16).reshape(C, RC, ROWS)
    for d in range(1, C):
        to = cpeer(d)
        go(remote(xt.at[to], xu.at[c, f], x1_send.at[d], x1_recv.at[d], (to, f)))
    xu[c, f] = xt[c]

    w_copies[1].wait()
    conv = conv + jnp.dot(
        x_rows[...].reshape(ROWS, D), w_ref[1], preferred_element_type=jnp.float32
    )
    spread_on(vu, v2_send, v2_recv)
    w_copies[2].wait()
    conv = conv + jnp.dot(after, w_ref[2], preferred_element_type=jnp.float32)

    scale = math.sqrt(2.0 / math.pi)
    square = conv * conv
    tanh = jnp.tanh(scale * conv * (1.0 + 0.044715 * square))
    cdf = 0.5 * (1.0 + tanh)
    slope[...] = cdf + (0.5 * scale) * conv * (1.0 - tanh * tanh) * (1.0 + 0.134145 * square)
    hidden = xf + conv * cdf
    pooled = jnp.sum(hidden.reshape(T, NB, D), axis=0) * (1.0 / T)
    pnorm = jnp.sqrt(jnp.sum(pooled * pooled, axis=1, keepdims=True) + 1e-06)
    unit = pooled / pnorm
    u_low = unit.astype(jnp.bfloat16)
    lanes = lax.broadcasted_iota(jnp.int32, (NB, F * NB), 1)
    mine = lanes == f * NB + lax.broadcasted_iota(jnp.int32, (NB, F * NB), 0)
    every_pos = jnp.broadcast_to(pos_ref[...].astype(jnp.float32), (NB, F * NB))
    pos_own = jnp.sum(jnp.where(mine, every_pos, 0.0), axis=1, keepdims=True)
    high = jnp.floor(pos_own * (1.0 / 128.0))
    lane = lax.broadcasted_iota(jnp.int32, (NB, 128), 1)
    split = jnp.where(lane < 64, high, pos_own - 128.0 * high)
    uu[c, f] = pack(u_low.astype(jnp.float32), split)
    for d in range(1, C):
        go(remote(uu.at[c, f], uu.at[c, f], u1_send.at[d], u1_recv.at[d], (cpeer(d), f)))

    spread_end(vu, v2_send, v2_recv)
    caps = C * F * NB
    vb[...] = unpack(vu[...], D)[0]
    logits = 10.0 * nt_dot(u_low, vb[...]) - 10.0
    ids = lax.broadcasted_iota(jnp.int32, (NB, caps), 1).astype(jnp.float32)
    match = jnp.where(pos_own == ids, 1.0, 0.0)
    coef = (10.0 * (1.0 / (1.0 + jnp.exp(-logits)) - match)).astype(jnp.bfloat16)
    du = jnp.dot(coef, vb[...], preferred_element_type=jnp.float32)
    dpooled = (du - unit * jnp.sum(unit * du, axis=1, keepdims=True)) / pnorm
    step = dpooled * (1.0 / T)
    dconv = (slope[...].reshape(T, NB, D) * step[None]).reshape(ROWS, D)
    dt[...] = dconv.T.astype(jnp.bfloat16).reshape(F, CC, ROWS)
    family = (f, beside, across, diagonal)
    for q in (2, 3, 1):
        to = family[q]
        go(remote(dt.at[to], dbuf.at[c, f], da_send.at[q], da_recv.at[q], (c, to)))
    dbuf[c, f] = dt[f]

    ways = (right, left)

    def block_at(way, hop):
        return ring_to_clip(lax.rem(pos + (C - hop if way == 0 else hop), C), C)

    def units_at(way, hop):
        if hop < half:
            return range(F)
        return range(F // 2) if way == 0 else range(F // 2, F)

    def forward(way, hop, q):
        slot = dbuf.at[block_at(way, hop), family[q]]
        go(
            remote(
                slot,
                slot,
                ring_send.at[way, hop, q],
                ring_recv.at[way, hop, q],
                (ways[way], f),
            )
        )

    def arrive(way, hop, q):
        slot = dbuf.at[block_at(way, hop), family[q]]
        remote(
            slot,
            slot,
            ring_send.at[way, hop - 1, q],
            ring_recv.at[way, hop - 1, q],
            (ways[way], f),
        ).wait_recv()

    def relay(hop, *which):
        for q in which:
            for way in range(2):
                if q in units_at(way, hop):
                    arrive(way, hop, q)
                    if hop < half and q in units_at(way, hop + 1):
                        forward(way, hop, q)

    def block_term(block):
        rhs = jnp.concatenate([dbuf[block, i] for i in range(F)], axis=1)
        return nt_dot(x3[block], rhs)

    def add_block(block, first=False):
        if first:
            acc[...] = block_term(block)
        else:
            acc[...] += block_term(block)

    for q in range(F):
        if q:
            source = family[q]
            slot = dbuf.at[c, source]
            remote(slot, slot, da_send.at[q], da_recv.at[q], (c, source)).wait_recv()
        for way in range(2):
            if q in units_at(way, 1):
                forward(way, 0, q)

    clip_arrive(xu, x1_send, x1_recv)
    spread(xu, x2_send, x2_recv)
    relay(1, 0)
    clip_arrive(uu, u1_send, u1_recv)
    spread(uu, u2_send, u2_recv)
    relay(1, 1, 2)
    spread_on(xu, x2_send, x2_recv)
    relay(1, 3)
    spread_end(xu, x2_send, x2_recv)
    row = lax.broadcasted_iota(jnp.int32, (ROWS, ROWS), 0)
    col = lax.broadcasted_iota(jnp.int32, (ROWS, ROWS), 1)
    later = jnp.where(row == col - NB, 1.0, 0.0)
    earlier = jnp.where(row == col + NB, 1.0, 0.0)
    moves = jnp.concatenate([later, earlier], axis=1).astype(jnp.bfloat16)

    def shift(block, carry):
        units = xu[block]
        moved = jnp.dot(
            units.reshape(F * RC, ROWS), moves, preferred_element_type=jnp.float32
        ).astype(jnp.bfloat16)
        for i in range(F):
            lanes = slice(i * ROWS, (i + 1) * ROWS)
            rows = slice(i * RC, (i + 1) * RC)
            x3[block, 0:RC, lanes] = moved[rows, :ROWS]
            x3[block, RC : 2 * RC, lanes] = units[i]
            x3[block, 2 * RC :, lanes] = moved[rows, ROWS:]
        return carry

    quarter = C // 4
    for q in range(4):
        lax.fori_loop(q * quarter, (q + 1) * quarter, shift, 0)
        relay(2, q)
    add_block(c, first=True)
    spread_on(uu, u2_send, u2_recv)
    add_block(block_at(0, 1))
    relay(3, 0)
    add_block(block_at(1, 1))
    relay(3, 1)
    add_block(block_at(0, 2))
    relay(3, 2)
    add_block(block_at(1, 2))
    relay(3, 3)
    spread_end(uu, u2_send, u2_recv)
    u_all, halves = unpack(uu[...], D)
    ub[...] = u_all
    pos_all = 128.0 * halves[:, :1] + halves[:, 64:65]
    turned = halves.T
    pos_row = 128.0 * turned[:1] + turned[64:65]
    first_id = (c * F + f) * NB
    own_ids = (first_id + lax.broadcasted_iota(jnp.int32, (NB, caps), 0)).astype(jnp.float32)
    match_own = jnp.where(pos_row == own_ids, 1.0, 0.0)
    logits_own = 10.0 * nt_dot(v_own, ub[...]) - 10.0
    coef_own = (10.0 * (1.0 / (1.0 + jnp.exp(-logits_own)) - match_own)).astype(jnp.bfloat16)
    dv = jnp.dot(coef_own, ub[...], preferred_element_type=jnp.float32)
    gc_ref[...] = (dv - vunit * jnp.sum(vunit * dv, axis=1, keepdims=True)) / cnorm

    every = 10.0 * nt_dot(ub[...], vb[...]) - 10.0
    all_ids = lax.broadcasted_iota(jnp.int32, (caps, caps), 1).astype(jnp.float32)
    signed = jnp.where(pos_all == all_ids, -every, every)
    soft = jnp.maximum(signed, 0.0) + jnp.log1p(jnp.exp(-jnp.abs(signed)))
    total = jnp.sum(jnp.sum(soft, axis=0, keepdims=True), axis=1, keepdims=True)
    loss_ref[...] = jnp.broadcast_to(total * (1.0 / caps), loss_ref.shape)

    add_block(block_at(0, 3))
    add_block(block_at(1, 3))
    relay(4, *range(F))
    gw_ref[...] = (acc[...] + block_term(block_at(0, 4))).reshape(3, RC, CC)
    for copy in sends:
        copy.wait_send()


def fused(C, F, frames, conv_weight, captions, positive):
    clip_dev, fr_dev, D = frames.shape
    NB = clip_dev // F
    ROWS = FRAMES * NB
    RC, CC = D // C, D // F
    half = C // 2
    blocks = frames.reshape(F, NB, fr_dev, D).transpose(0, 2, 1, 3).reshape(F, fr_dev * NB, D)
    vmem = pl.BlockSpec(memory_space=pltpu.VMEM)
    hbm = pl.BlockSpec(memory_space=pltpu.HBM)
    dma = pltpu.SemaphoreType.DMA
    bf16, f32 = jnp.bfloat16, jnp.float32
    caps = C * F * NB
    loss, grad_weight, grad_captions = pl.pallas_call(
        functools.partial(fused_kernel, C, F),
        out_shape=(
            jax.ShapeDtypeStruct((8, 128), f32),
            jax.ShapeDtypeStruct((3, RC, CC), f32),
            jax.ShapeDtypeStruct((NB, D), f32),
        ),
        in_specs=[hbm, hbm, hbm, hbm],
        out_specs=(vmem, vmem, vmem),
        scratch_shapes=[
            pltpu.VMEM((NB, D), bf16),
            pltpu.VMEM((1, clip_dev), jnp.int32),
            pltpu.VMEM((3, D, D), bf16),
            pltpu.VMEM((F, ROWS // F, D), bf16),
            pltpu.VMEM((C, RC, ROWS), bf16),
            pltpu.VMEM((C, F, RC, ROWS), bf16),
            pltpu.VMEM((C, 3 * RC, F * ROWS), bf16),
            pltpu.VMEM((C, F, 2 * NB, (D + 128) // 2), bf16),
            pltpu.VMEM((caps, D), bf16),
            pltpu.VMEM((C, F, 2 * NB, (D + 128) // 2), bf16),
            pltpu.VMEM((caps, D), bf16),
            pltpu.VMEM((ROWS, D), f32),
            pltpu.VMEM((F, CC, ROWS), bf16),
            pltpu.VMEM((C, F, CC, ROWS), bf16),
            pltpu.VMEM((3 * RC, CC), f32),
            dma,
            dma,
            dma,
            dma((3,)),
            dma((F,)),
            dma((F,)),
            dma((C,)),
            dma((C,)),
            dma((F,)),
            dma((F,)),
            dma((C,)),
            dma((C,)),
            dma((F,)),
            dma((F,)),
            dma((C,)),
            dma((C,)),
            dma((F,)),
            dma((F,)),
            dma((F,)),
            dma((F,)),
            dma((2, half, F)),
            dma((2, half, F)),
        ],
        compiler_params=pltpu.CompilerParams(
            collective_id=0, has_side_effects=True, vmem_limit_bytes=52 * 1024 * 1024
        ),
        cost_estimate=pl.CostEstimate(
            flops=4 * 3 * ROWS * D * D, bytes_accessed=8 * D * D, transcendentals=ROWS * D
        ),
    )(blocks, conv_weight, captions, positive.reshape(1, clip_dev))
    return loss[0, 0], grad_weight, grad_captions


def fits(C, F, frames, captions):
    clip_dev, fr_dev, D = frames.shape
    clips = clip_dev // F
    return (
        C == 8
        and F == 4
        and clips == 8
        and clip_dev % F == 0
        and captions.shape[0] == clips
        and fr_dev * F == FRAMES
        and D % (16 * C) == 0
        and D % 128 == 0
    )


def on_device(frames, conv_weight, captions, positive):
    C, F = lax.axis_size("clip"), lax.axis_size("frame")
    if fits(C, F, frames, captions):
        return fused(C, F, frames, conv_weight, captions, positive)
    return plain(frames, conv_weight, captions, positive)


def solution(mesh):
    placed = (P("clip", "frame", None), P(), P(("clip", "frame"), None), P("clip"))
    return jax.shard_map(
        on_device,
        mesh=mesh,
        in_specs=placed,
        out_specs=(P(), P(None, "clip", "frame"), P(("clip", "frame"), None)),
        check_vma=False,
    )
```

```python
import functools
import math

import jax
import jax.numpy as jnp
from jax import lax
from jax.experimental import pallas as pl
from jax.experimental.pallas import tpu as pltpu
from jax.sharding import PartitionSpec as P

FRAMES = 16


def with_halo(block, sides, width):
    for axis, dim in sides:
        count = lax.axis_size(axis)
        forward = [(i, i + 1) for i in range(count - 1)]
        backward = [(target, source) for source, target in forward]
        low = lax.ppermute(
            lax.slice_in_dim(block, block.shape[dim] - width, None, axis=dim), axis, forward
        )
        high = lax.ppermute(lax.slice_in_dim(block, 0, width, axis=dim), axis, backward)
        block = jnp.concatenate([low, block, high], axis=dim)
    return block


def plain(frames, conv_weight, captions, positive):
    clip_dev, fr_dev, width = frames.shape
    rows = clip_dev * fr_dev
    padded = with_halo(frames, (("frame", 1),), 1)
    shifted = [padded[:, k : k + fr_dev].reshape(rows, width) for k in range(3)]
    conv = jnp.dot(shifted[0], conv_weight[0], preferred_element_type=jnp.float32)
    conv = conv + jnp.dot(shifted[1], conv_weight[1], preferred_element_type=jnp.float32)
    conv = conv + jnp.dot(shifted[2], conv_weight[2], preferred_element_type=jnp.float32)
    hidden = frames.reshape(rows, width).astype(jnp.float32) + jax.nn.gelu(conv)
    partial_pool = jnp.sum(hidden.reshape(clip_dev, fr_dev, width), axis=1)
    pooled = lax.psum(partial_pool, "frame") / FRAMES
    pnorm = jnp.sqrt(jnp.sum(pooled * pooled, axis=1, keepdims=True) + 1e-06)
    unit = pooled / pnorm
    u_low = unit.astype(jnp.bfloat16)
    capf = captions.astype(jnp.float32)
    cnorm = jnp.sqrt(jnp.sum(capf * capf, axis=1, keepdims=True) + 1e-06)
    vunit = capf / cnorm
    v_low = vunit.astype(jnp.bfloat16)
    cap_dev = captions.shape[0]
    frame_pos = lax.axis_index("frame")
    piece = lax.all_gather(v_low, "clip", axis=0, tiled=True)
    count = piece.shape[0]
    place = jnp.arange(count, dtype=jnp.int32)
    ids = place // cap_dev * clip_dev + frame_pos * cap_dev + place % cap_dev
    logits = (
        10.0
        * lax.dot_general(
            u_low, piece, (((1,), (1,)), ((), ())), preferred_element_type=jnp.float32
        )
        - 10.0
    )
    match = (positive[:, None] == ids[None, :]).astype(jnp.float32)
    sign = 2.0 * match - 1.0
    total = jnp.sum(jax.nn.softplus(-sign * logits))
    coef = (10.0 * (jax.nn.sigmoid(logits) - match)).astype(jnp.bfloat16)
    du_acc = jnp.dot(coef, piece, preferred_element_type=jnp.float32)
    dv_piece = lax.dot_general(
        coef, u_low, (((0,), (0,)), ((), ())), preferred_element_type=jnp.float32
    )
    total, du_part, dv_all = (total, du_acc, dv_piece)
    dv_mine = lax.psum_scatter(dv_all, "clip", scatter_dimension=0, tiled=True)
    grad_captions = (dv_mine - vunit * jnp.sum(vunit * dv_mine, axis=1, keepdims=True)) / cnorm
    loss = lax.psum(total, ("clip", "frame")) / (clip_dev * lax.axis_size("clip"))
    du_full = lax.psum(du_part, "frame")
    dpooled = (du_full - unit * jnp.sum(unit * du_full, axis=1, keepdims=True)) / pnorm
    dhidden = jnp.broadcast_to((dpooled / FRAMES)[:, None, :], (clip_dev, fr_dev, width)).reshape(
        rows, width
    )
    _, pull = jax.vjp(jax.nn.gelu, conv)
    dconv = pull(dhidden)[0].astype(jnp.bfloat16).reshape(clip_dev, fr_dev, width)
    dconv_cols = lax.all_to_all(dconv, "frame", split_axis=2, concat_axis=1, tiled=True)
    block = fr_dev + 2
    col_width = dconv_cols.shape[2]
    every_block = lax.all_gather(padded, "frame", axis=1, tiled=True)
    groups = every_block.shape[1] // block
    blocks = every_block.reshape(clip_dev, groups, block, width)
    grads = dconv_cols.reshape(clip_dev, groups, fr_dev, col_width)
    parts = [
        jnp.einsum(
            "cgtd,cgte->de", blocks[:, :, k : k + fr_dev], grads, preferred_element_type=jnp.float32
        )
        for k in range(3)
    ]
    terms = jnp.stack(parts)
    grad_weight = lax.psum_scatter(terms, "clip", scatter_dimension=1, tiled=True)
    return (loss, grad_weight, grad_captions)


MESH = pl.DeviceIdType.MESH


def remote(src, dst, send_sem, recv_sem, device):
    return pltpu.make_async_remote_copy(
        src_ref=src,
        dst_ref=dst,
        send_sem=send_sem,
        recv_sem=recv_sem,
        device_id=device,
        device_id_type=MESH,
    )


def nt_dot(a, b):
    return lax.dot_general(a, b, (((1,), (1,)), ((), ())), preferred_element_type=jnp.float32)


def ring_to_clip(r, count):
    high = r // (count // 2)
    return 2 * r + high * (2 * count - 1 - 4 * r)


def pack(rows, extra):
    cut = (rows.shape[1] + extra.shape[1]) // 2
    bottom = jnp.concatenate([rows[:, cut:], extra], axis=1)
    return jnp.concatenate([rows[:, :cut], bottom], axis=0).astype(jnp.bfloat16)


def unpack(units, width):
    C, F, tall, cut = units.shape
    flat = units.reshape(C * F, tall, cut).astype(jnp.float32)
    top = flat[:, : tall // 2].reshape(C * F * tall // 2, cut)
    bottom = flat[:, tall // 2 :].reshape(C * F * tall // 2, cut)
    rows = jnp.concatenate([top, bottom[:, : width - cut]], axis=1)
    return rows.astype(jnp.bfloat16), bottom[:, width - cut :]


def fused_kernel(
    C,
    F,
    frames_ref,
    w_hbm,
    cap_hbm,
    pos_hbm,
    loss_ref,
    gw_ref,
    gc_ref,
    cap_ref,
    pos_ref,
    w_ref,
    x_rows,
    xt,
    xu,
    x3,
    vu,
    vb,
    uu,
    ub,
    slope,
    dt,
    dbuf,
    acc,
    cap_sem,
    pos_sem,
    own_sem,
    w_sem,
    fr_send,
    fr_recv,
    v1_send,
    v1_recv,
    v2_send,
    v2_recv,
    x1_send,
    x1_recv,
    x2_send,
    x2_recv,
    u1_send,
    u1_recv,
    u2_send,
    u2_recv,
    da_send,
    da_recv,
    ring_send,
    ring_recv,
):
    D = cap_ref.shape[1]
    NB = cap_ref.shape[0]
    T = FRAMES
    ROWS = T * NB
    part = ROWS // F
    RC = D // C
    CC = D // F
    c = lax.axis_index("clip")
    f = lax.axis_index("frame")
    half = C // 2
    z = c // 2
    pos = z + (c - 2 * z) * (C - 1 - 2 * z)
    right = ring_to_clip(lax.rem(pos + 1, C), C)
    left = ring_to_clip(lax.rem(pos + C - 1, C), C)

    cap_copy = pltpu.make_async_copy(cap_hbm, cap_ref, cap_sem)
    cap_copy.start()
    own_copy = pltpu.make_async_copy(frames_ref.at[f], x_rows.at[f], own_sem)
    own_copy.start()
    pos_copy = pltpu.make_async_copy(pos_hbm, pos_ref, pos_sem)
    pos_copy.start()
    w_copies = [pltpu.make_async_copy(w_hbm.at[k], w_ref.at[k], w_sem.at[k]) for k in range(3)]
    for copy in w_copies:
        copy.start()

    def cpeer(d):
        return lax.rem(c + d, C)

    def fpeer(d):
        return lax.rem(f + d, F)

    barrier = pltpu.get_barrier_semaphore()
    for d in range(1, C):
        pl.semaphore_signal(barrier, inc=1, device_id=(cpeer(d), f), device_id_type=MESH)
    for d in range(1, F):
        pl.semaphore_signal(barrier, inc=1, device_id=(c, fpeer(d)), device_id_type=MESH)

    cap_copy.wait()
    capf = cap_ref[...].astype(jnp.float32)
    cnorm = jnp.sqrt(jnp.sum(capf * capf, axis=1, keepdims=True) + 1e-06)
    vunit = capf / cnorm
    v_own = vunit.astype(jnp.bfloat16)
    vu[c, f] = pack(v_own.astype(jnp.float32), jnp.zeros((NB, 128), jnp.float32))
    pl.semaphore_wait(barrier, C + F - 2)

    sends = []

    def go(copy):
        copy.start()
        sends.append(copy)

    across = lax.rem(f + F // 2, F)
    beside = f + 1 - 2 * lax.rem(f, 2)
    diagonal = lax.rem(beside + F // 2, F)

    def spread(array, send_sem, recv_sem):
        slab = array.at[:, f]
        go(remote(slab, slab, send_sem.at[0], recv_sem.at[0], (c, across)))
        go(remote(slab, slab, send_sem.at[1], recv_sem.at[1], (c, beside)))

    def spread_on(array, send_sem, recv_sem):
        slab = array.at[:, across]
        remote(slab, slab, send_sem.at[0], recv_sem.at[0], (c, across)).wait_recv()
        go(remote(slab, slab, send_sem.at[2], recv_sem.at[2], (c, beside)))

    def spread_end(array, send_sem, recv_sem):
        for i, source in ((1, beside), (2, diagonal)):
            slab = array.at[:, source]
            remote(slab, slab, send_sem.at[i], recv_sem.at[i], (c, beside)).wait_recv()

    def clip_arrive(array, send_sem, recv_sem):
        for d in range(1, C):
            source = cpeer(C - d)
            slot = array.at[source, f]
            remote(slot, slot, send_sem.at[d], recv_sem.at[d], (source, f)).wait_recv()

    for d in range(1, F):
        go(
            remote(
                frames_ref.at[fpeer(d)],
                x_rows.at[f],
                fr_send.at[d],
                fr_recv.at[d],
                (c, fpeer(d)),
            )
        )
    for d in range(1, C):
        go(remote(vu.at[c, f], vu.at[c, f], v1_send.at[d], v1_recv.at[d], (cpeer(d), f)))

    for d in range(1, F):
        source = fpeer(F - d)
        remote(
            x_rows.at[source], x_rows.at[source], fr_send.at[d], fr_recv.at[d], (c, source)
        ).wait_recv()
    own_copy.wait()
    pos_copy.wait()
    xf = x_rows[...].reshape(ROWS, D).astype(jnp.float32)
    edge = jnp.zeros((NB, D), jnp.float32)
    before = jnp.concatenate([edge, xf[: ROWS - NB]], axis=0).astype(jnp.bfloat16)
    after = jnp.concatenate([xf[NB:], edge], axis=0).astype(jnp.bfloat16)
    w_copies[0].wait()
    clip_arrive(vu, v1_send, v1_recv)
    spread(vu, v2_send, v2_recv)
    conv = jnp.dot(before, w_ref[0], preferred_element_type=jnp.float32)
    xt[...] = xf.T.astype(jnp.bfloat16).reshape(C, RC, ROWS)
    for d in range(1, C):
        to = cpeer(d)
        go(remote(xt.at[to], xu.at[c, f], x1_send.at[d], x1_recv.at[d], (to, f)))
    xu[c, f] = xt[c]

    w_copies[1].wait()
    conv = conv + jnp.dot(
        x_rows[...].reshape(ROWS, D), w_ref[1], preferred_element_type=jnp.float32
    )
    spread_on(vu, v2_send, v2_recv)
    w_copies[2].wait()
    conv = conv + jnp.dot(after, w_ref[2], preferred_element_type=jnp.float32)

    scale = math.sqrt(2.0 / math.pi)
    square = conv * conv
    tanh = jnp.tanh(scale * conv * (1.0 + 0.044715 * square))
    cdf = 0.5 * (1.0 + tanh)
    slope[...] = cdf + (0.5 * scale) * conv * (1.0 - tanh * tanh) * (1.0 + 0.134145 * square)
    hidden = xf + conv * cdf
    pooled = jnp.sum(hidden.reshape(T, NB, D), axis=0) * (1.0 / T)
    pnorm = jnp.sqrt(jnp.sum(pooled * pooled, axis=1, keepdims=True) + 1e-06)
    unit = pooled / pnorm
    u_low = unit.astype(jnp.bfloat16)
    lanes = lax.broadcasted_iota(jnp.int32, (NB, F * NB), 1)
    mine = lanes == f * NB + lax.broadcasted_iota(jnp.int32, (NB, F * NB), 0)
    every_pos = jnp.broadcast_to(pos_ref[...].astype(jnp.float32), (NB, F * NB))
    pos_own = jnp.sum(jnp.where(mine, every_pos, 0.0), axis=1, keepdims=True)
    high = jnp.floor(pos_own * (1.0 / 128.0))
    lane = lax.broadcasted_iota(jnp.int32, (NB, 128), 1)
    split = jnp.where(lane < 64, high, pos_own - 128.0 * high)
    uu[c, f] = pack(u_low.astype(jnp.float32), split)
    for d in range(1, C):
        go(remote(uu.at[c, f], uu.at[c, f], u1_send.at[d], u1_recv.at[d], (cpeer(d), f)))

    spread_end(vu, v2_send, v2_recv)
    caps = C * F * NB
    vb[...] = unpack(vu[...], D)[0]
    logits = 10.0 * nt_dot(u_low, vb[...]) - 10.0
    ids = lax.broadcasted_iota(jnp.int32, (NB, caps), 1).astype(jnp.float32)
    match = jnp.where(pos_own == ids, 1.0, 0.0)
    coef = (10.0 * (1.0 / (1.0 + jnp.exp(-logits)) - match)).astype(jnp.bfloat16)
    du = jnp.dot(coef, vb[...], preferred_element_type=jnp.float32)
    dpooled = (du - unit * jnp.sum(unit * du, axis=1, keepdims=True)) / pnorm
    step = dpooled * (1.0 / T)
    dconv = (slope[...].reshape(T, NB, D) * step[None]).reshape(ROWS, D)
    dt[...] = dconv.T.astype(jnp.bfloat16).reshape(F, CC, ROWS)
    family = (f, beside, across, diagonal)
    for q in (2, 3, 1):
        to = family[q]
        go(remote(dt.at[to], dbuf.at[c, f], da_send.at[q], da_recv.at[q], (c, to)))
    dbuf[c, f] = dt[f]

    ways = (right, left)

    def block_at(way, hop):
        return ring_to_clip(lax.rem(pos + (C - hop if way == 0 else hop), C), C)

    def units_at(way, hop):
        if hop < half:
            return range(F)
        return range(F // 2) if way == 0 else range(F // 2, F)

    def forward(way, hop, q):
        slot = dbuf.at[block_at(way, hop), family[q]]
        go(
            remote(
                slot,
                slot,
                ring_send.at[way, hop, q],
                ring_recv.at[way, hop, q],
                (ways[way], f),
            )
        )

    def arrive(way, hop, q):
        slot = dbuf.at[block_at(way, hop), family[q]]
        remote(
            slot,
            slot,
            ring_send.at[way, hop - 1, q],
            ring_recv.at[way, hop - 1, q],
            (ways[way], f),
        ).wait_recv()

    def relay(hop, *which):
        for q in which:
            for way in range(2):
                if q in units_at(way, hop):
                    arrive(way, hop, q)
                    if hop < half and q in units_at(way, hop + 1):
                        forward(way, hop, q)

    def block_term(block):
        rhs = jnp.concatenate([dbuf[block, i] for i in range(F)], axis=1)
        return nt_dot(x3[block], rhs)

    def add_block(block, first=False):
        if first:
            acc[...] = block_term(block)
        else:
            acc[...] += block_term(block)

    for q in range(F):
        if q == 2:
            clip_arrive(xu, x1_send, x1_recv)
            spread(xu, x2_send, x2_recv)
        if q:
            source = family[q]
            slot = dbuf.at[c, source]
            remote(slot, slot, da_send.at[q], da_recv.at[q], (c, source)).wait_recv()
        for way in range(2):
            if q in units_at(way, 1):
                forward(way, 0, q)

    relay(1, 0)
    clip_arrive(uu, u1_send, u1_recv)
    spread(uu, u2_send, u2_recv)
    relay(1, 1)
    spread_on(xu, x2_send, x2_recv)
    relay(1, 2, 3)
    spread_end(xu, x2_send, x2_recv)
    row = lax.broadcasted_iota(jnp.int32, (ROWS, ROWS), 0)
    col = lax.broadcasted_iota(jnp.int32, (ROWS, ROWS), 1)
    later = jnp.where(row == col - NB, 1.0, 0.0)
    earlier = jnp.where(row == col + NB, 1.0, 0.0)
    moves = jnp.concatenate([later, earlier], axis=1).astype(jnp.bfloat16)

    def shift(block, carry):
        units = xu[block]
        moved = jnp.dot(
            units.reshape(F * RC, ROWS), moves, preferred_element_type=jnp.float32
        ).astype(jnp.bfloat16)
        for i in range(F):
            lanes = slice(i * ROWS, (i + 1) * ROWS)
            rows = slice(i * RC, (i + 1) * RC)
            x3[block, 0:RC, lanes] = moved[rows, :ROWS]
            x3[block, RC : 2 * RC, lanes] = units[i]
            x3[block, 2 * RC :, lanes] = moved[rows, ROWS:]
        return carry

    quarter = C // 4
    for q in range(4):
        lax.fori_loop(q * quarter, (q + 1) * quarter, shift, 0)
        relay(2, q)
    add_block(c, first=True)
    spread_on(uu, u2_send, u2_recv)
    add_block(block_at(0, 1))
    relay(3, 0)
    add_block(block_at(1, 1))
    relay(3, 1)
    add_block(block_at(0, 2))
    relay(3, 2)
    add_block(block_at(1, 2))
    relay(3, 3)
    spread_end(uu, u2_send, u2_recv)
    u_all, halves = unpack(uu[...], D)
    ub[...] = u_all
    pos_all = 128.0 * halves[:, :1] + halves[:, 64:65]
    turned = halves.T
    pos_row = 128.0 * turned[:1] + turned[64:65]
    first_id = (c * F + f) * NB
    own_ids = (first_id + lax.broadcasted_iota(jnp.int32, (NB, caps), 0)).astype(jnp.float32)
    match_own = jnp.where(pos_row == own_ids, 1.0, 0.0)
    logits_own = 10.0 * nt_dot(v_own, ub[...]) - 10.0
    coef_own = (10.0 * (1.0 / (1.0 + jnp.exp(-logits_own)) - match_own)).astype(jnp.bfloat16)
    dv = jnp.dot(coef_own, ub[...], preferred_element_type=jnp.float32)
    gc_ref[...] = (dv - vunit * jnp.sum(vunit * dv, axis=1, keepdims=True)) / cnorm

    every = 10.0 * nt_dot(ub[...], vb[...]) - 10.0
    all_ids = lax.broadcasted_iota(jnp.int32, (caps, caps), 1).astype(jnp.float32)
    signed = jnp.where(pos_all == all_ids, -every, every)
    soft = jnp.maximum(signed, 0.0) + jnp.log1p(jnp.exp(-jnp.abs(signed)))
    total = jnp.sum(jnp.sum(soft, axis=0, keepdims=True), axis=1, keepdims=True)
    loss_ref[...] = jnp.broadcast_to(total * (1.0 / caps), loss_ref.shape)

    add_block(block_at(0, 3))
    add_block(block_at(1, 3))
    relay(4, *range(F))
    gw_ref[...] = (acc[...] + block_term(block_at(0, 4))).reshape(3, RC, CC)
    for copy in sends:
        copy.wait_send()


def fused(C, F, frames, conv_weight, captions, positive):
    clip_dev, fr_dev, D = frames.shape
    NB = clip_dev // F
    ROWS = FRAMES * NB
    RC, CC = D // C, D // F
    half = C // 2
    blocks = frames.reshape(F, NB, fr_dev, D).transpose(0, 2, 1, 3).reshape(F, fr_dev * NB, D)
    vmem = pl.BlockSpec(memory_space=pltpu.VMEM)
    hbm = pl.BlockSpec(memory_space=pltpu.HBM)
    dma = pltpu.SemaphoreType.DMA
    bf16, f32 = jnp.bfloat16, jnp.float32
    caps = C * F * NB
    loss, grad_weight, grad_captions = pl.pallas_call(
        functools.partial(fused_kernel, C, F),
        out_shape=(
            jax.ShapeDtypeStruct((8, 128), f32),
            jax.ShapeDtypeStruct((3, RC, CC), f32),
            jax.ShapeDtypeStruct((NB, D), f32),
        ),
        in_specs=[hbm, hbm, hbm, hbm],
        out_specs=(vmem, vmem, vmem),
        scratch_shapes=[
            pltpu.VMEM((NB, D), bf16),
            pltpu.VMEM((1, clip_dev), jnp.int32),
            pltpu.VMEM((3, D, D), bf16),
            pltpu.VMEM((F, ROWS // F, D), bf16),
            pltpu.VMEM((C, RC, ROWS), bf16),
            pltpu.VMEM((C, F, RC, ROWS), bf16),
            pltpu.VMEM((C, 3 * RC, F * ROWS), bf16),
            pltpu.VMEM((C, F, 2 * NB, (D + 128) // 2), bf16),
            pltpu.VMEM((caps, D), bf16),
            pltpu.VMEM((C, F, 2 * NB, (D + 128) // 2), bf16),
            pltpu.VMEM((caps, D), bf16),
            pltpu.VMEM((ROWS, D), f32),
            pltpu.VMEM((F, CC, ROWS), bf16),
            pltpu.VMEM((C, F, CC, ROWS), bf16),
            pltpu.VMEM((3 * RC, CC), f32),
            dma,
            dma,
            dma,
            dma((3,)),
            dma((F,)),
            dma((F,)),
            dma((C,)),
            dma((C,)),
            dma((F,)),
            dma((F,)),
            dma((C,)),
            dma((C,)),
            dma((F,)),
            dma((F,)),
            dma((C,)),
            dma((C,)),
            dma((F,)),
            dma((F,)),
            dma((F,)),
            dma((F,)),
            dma((2, half, F)),
            dma((2, half, F)),
        ],
        compiler_params=pltpu.CompilerParams(
            collective_id=0, has_side_effects=True, vmem_limit_bytes=52 * 1024 * 1024
        ),
        cost_estimate=pl.CostEstimate(
            flops=4 * 3 * ROWS * D * D, bytes_accessed=8 * D * D, transcendentals=ROWS * D
        ),
    )(blocks, conv_weight, captions, positive.reshape(1, clip_dev))
    return loss[0, 0], grad_weight, grad_captions


def fits(C, F, frames, captions):
    clip_dev, fr_dev, D = frames.shape
    clips = clip_dev // F
    return (
        C == 8
        and F == 4
        and clips == 8
        and clip_dev % F == 0
        and captions.shape[0] == clips
        and fr_dev * F == FRAMES
        and D % (16 * C) == 0
        and D % 128 == 0
    )


def on_device(frames, conv_weight, captions, positive):
    C, F = lax.axis_size("clip"), lax.axis_size("frame")
    if fits(C, F, frames, captions):
        return fused(C, F, frames, conv_weight, captions, positive)
    return plain(frames, conv_weight, captions, positive)


def solution(mesh):
    placed = (P("clip", "frame", None), P(), P(("clip", "frame"), None), P("clip"))
    return jax.shard_map(
        on_device,
        mesh=mesh,
        in_specs=placed,
        out_specs=(P(), P(None, "clip", "frame"), P(("clip", "frame"), None)),
        check_vma=False,
    )
```
